32 devices in a mesh: req: 8 (over y, x, core), head: 4 (over z).
Axes of the slice: x: 2, y: 2, z: 4, core: 2. Of those that a mesh axis runs over, the one named last changes fastest.
Arguments:
- tokens: bfloat16 [16384, 2048], P(('req', 'head')), may hold values from -6 to 6
- input_gain: float32 [2048], replicated, may hold values from 0.1 to 1.9
- w_query: bfloat16 [2048, 2048], replicated, may hold values from -0.125 to 0.125
- w_keyval: bfloat16 [2048, 1024], replicated, may hold values from -0.125 to 0.125
- query_gain: float32 [256], replicated, may hold values from 0.1 to 1.9
- key_gain: float32 [256], replicated, may hold values from 0.1 to 1.9
- w_output: bfloat16 [2048, 2048], P('req'), may hold values from -0.125 to 0.125
- laurel_left: bfloat16 [2048, 64], replicated, may hold values from -0.125 to 0.125
- laurel_right: bfloat16 [64, 2048], replicated, may hold values from -0.75 to 0.75
- laurel_gain: float32 [2048], replicated, may hold values from 0.1 to 1.9
- post_gain: float32 [2048], replicated, may hold values from 0.1 to 1.9
- cache_pool: bfloat16 [512, 64, 1024], P('req'), may hold values from -200 to 200, as said below
- page_table: int32 [32, 16], replicated, may hold values from 0 to 63, as said below
- cached_len: int32 [32], replicated, may hold values from 0 to 1024, as said below
- slot_of: int32 [32], replicated, may hold values from 0 to 31, as said below
Outputs:
- mixed: bfloat16 [16384, 2048], P(('req', 'head'))
The draws below stay inside these ranges and needn't reach their ends.
Inputs may be any that keep to these rules, and one draw needn't show every extreme that they name: slot_of is a permutation of the 32 requests onto slots. Request i's pages lie in group i // 4. In each group exactly one request is served by the group before it and exactly one by the group after it (group indices cyclic over 8); all others are served by their own group. `page_table`: page p of request i holds its cached positions p*64 to (p+1)*64 - 1; the rows of the 4 requests of one group together name each of that group's 64 pages once. `cached_len`: at least one request that changes group has exactly 1024 cached positions, and some request has none. `cache_pool`: stored keys (already normalized and rotated) and values; entries past a request's cached length are arbitrary.
All inputs are finite; a program needn't handle non-finite values.
Results may differ from the reference program's by a relative error of at most 0.012.
The reference program's roundings to bfloat16 on the way (of `normed`, `query`, `key`, `value`, `weights`, `attended` and `low`) count: a program that leaves them out, or rounds other values in their place, can miss the bound.
Values may be sent and summed in bfloat16 or wider, within the bound.
No kernel may reach another device: no remote copies, remote signals or barrier semaphores. Data moves between devices by JAX's collectives and lax.ppermute only.
A program may use at most 128 MiB of HBM per device.

```python
import math
import jax
import jax.numpy as jnp
from jax import lax

D = 2048
NH = 8
KVH = 2
HD = 256
RANK = 64
REQ_DEV = 4
CH = 512
LMAX = 1024
PAGE = 64
MAXP = 16
POOL = 64
GROUPS = 8
NREQ = 32
NTOK = 16384


def mover_order(key):
    groups = NREQ // REQ_DEV
    subkeys = jax.random.split(jax.random.fold_in(key, 7), groups)
    return jax.vmap(lambda subkey: jax.random.permutation(subkey, REQ_DEV))(subkeys).astype(jnp.int32)


def draw_slot_of(key, part):
    groups = NREQ // REQ_DEV
    order = mover_order(key)
    group_ids = jnp.arange(groups, dtype=jnp.int32)
    staying = group_ids[:, None] * REQ_DEV + order[:, 2:]
    from_after = ((group_ids + 1) % groups * REQ_DEV + jnp.roll(order[:, 0], -1))[:, None]
    from_before = ((group_ids + groups - 1) % groups * REQ_DEV + jnp.roll(order[:, 1], 1))[:, None]
    members = jnp.concatenate([staying, from_after, from_before], axis=1)
    subkeys = jax.random.split(jax.random.fold_in(key, 9), groups)
    shuffle = jax.vmap(lambda subkey: jax.random.permutation(subkey, REQ_DEV))(subkeys).astype(jnp.int32)
    placed = jnp.take_along_axis(members, shuffle, axis=1)
    return jnp.zeros((NREQ,), jnp.int32).at[placed.reshape(-1)].set(jnp.arange(NREQ, dtype=jnp.int32))


def draw_cached_len(key, part):
    groups = NREQ // REQ_DEV
    order = mover_order(key)
    lengths = jax.random.randint(jax.random.fold_in(key, 3), (NREQ,), LMAX // 2, LMAX + 1).astype(jnp.int32)
    chosen = jax.random.randint(jax.random.fold_in(key, 5), (), 0, groups)
    lengths = lengths.at[chosen * REQ_DEV + order[chosen, 0]].set(LMAX)
    other = (chosen + 1) % groups
    lengths = lengths.at[other * REQ_DEV + order[other, REQ_DEV - 1]].set(0)
    return lengths


def draw_page_table(key, part):
    groups = NREQ // REQ_DEV
    subkeys = jax.random.split(jax.random.fold_in(key, 13), groups)
    pages = jax.vmap(lambda subkey: jax.random.permutation(subkey, POOL))(subkeys)
    return pages.reshape(NREQ, MAXP).astype(jnp.int32)


def draw_cache_pool(key, part):
    rows = GROUPS * POOL
    values = jnp.clip(jax.random.normal(jax.random.fold_in(key, 24), (rows, PAGE, 2 * KVH, HD), jnp.float32), -6.0, 6.0)
    return values.reshape(rows, PAGE, 2 * KVH * HD).astype(jnp.bfloat16)


def level_of(rng, extent, shards, low, top_value):
    level = 1.0
    for axis_at, blocks in shards:
        steps = jax.random.uniform(jax.random.fold_in(jax.random.fold_in(rng, 6), axis_at), (blocks,), jnp.float32, low / len(shards), top_value / len(shards))
        level = level * jnp.repeat(jnp.exp(steps), extent[axis_at] // blocks).reshape((-1,) + (1,) * (len(extent) - 1 - axis_at))
    return level


def normal_values(stream_key, shape, width, most, pieces=(), kind=jnp.bfloat16):
    gain = level_of(stream_key, shape, pieces, -0.22, 0.18) if pieces else 1.0
    values = jax.random.normal(stream_key, shape, jnp.float32) * width * gain
    return jnp.minimum(jnp.maximum(values, -most), most).astype(kind)


def setup_inputs(seed: int = 0) -> dict:
    streams_of = jax.random.split(jax.random.key(seed), 16)
    return {
        "tokens": normal_values(streams_of[0], (NTOK, D), 1.0, 6.0, ((0, 32),)),
        "input_gain": jnp.clip(1.0 + 0.18 * jax.random.normal(streams_of[1], (D,), jnp.float32), 0.1, 1.9),
        "w_query": normal_values(streams_of[2], (D, NH * HD), D ** -0.5, 0.125),
        "w_keyval": normal_values(streams_of[3], (D, 2 * KVH * HD), D ** -0.5, 0.125),
        "query_gain": jnp.clip(1.0 + 0.18 * jax.random.normal(streams_of[4], (HD,), jnp.float32), 0.1, 1.9),
        "key_gain": jnp.clip(1.0 + 0.18 * jax.random.normal(streams_of[5], (HD,), jnp.float32), 0.1, 1.9),
        "w_output": normal_values(streams_of[6], (NH * HD, D), (NH * HD) ** -0.5, 0.125, ((0, 8),)),
        "laurel_left": normal_values(streams_of[7], (D, RANK), D ** -0.5, 0.125),
        "laurel_right": normal_values(streams_of[8], (RANK, D), RANK ** -0.5, 0.75),
        "laurel_gain": jnp.clip(1.0 + 0.18 * jax.random.normal(streams_of[9], (D,), jnp.float32), 0.1, 1.9),
        "post_gain": jnp.clip(1.0 + 0.18 * jax.random.normal(streams_of[10], (D,), jnp.float32), 0.1, 1.9),
        "cache_pool": draw_cache_pool(jax.random.fold_in(streams_of[15], 71), 0),
        "page_table": draw_page_table(jax.random.fold_in(streams_of[15], 71), 0),
        "cached_len": draw_cached_len(jax.random.fold_in(streams_of[15], 71), 0),
        "slot_of": draw_slot_of(jax.random.fold_in(streams_of[15], 71), 0),
    }


epsilon = 1e-06

def normalize(values_in):
    return values_in * lax.rsqrt(lax.optimization_barrier(jnp.mean(values_in * values_in, axis=-1, keepdims=True)) + epsilon)

def rotate(values_in, position):
    half = values_in.shape[-1] // 2
    exponent = jnp.arange(half, dtype=jnp.float32) * (2.0 / values_in.shape[-1])
    inverse = jnp.power(jnp.float32(1000000.0), -exponent)
    angle = position.astype(jnp.float32)[:, None] * inverse[None, :]
    cosine = jnp.cos(angle)[:, None, :]
    sine = jnp.sin(angle)[:, None, :]
    first_half = values_in[..., :half]
    second_half = values_in[..., half:]
    return jnp.concatenate([first_half * cosine - second_half * sine, second_half * cosine + first_half * sine], axis=-1)

def reference(tokens, input_gain, w_query, w_keyval, query_gain, key_gain, w_output, laurel_left, laurel_right, laurel_gain, post_gain, cache_pool, page_table, cached_len, slot_of):
    inputs = tokens.astype(jnp.float32)
    normed = (normalize(inputs) * input_gain).astype(jnp.bfloat16)
    query_raw = jnp.dot(normed, w_query, preferred_element_type=jnp.float32)
    keyval_raw = jnp.dot(normed, w_keyval, preferred_element_type=jnp.float32)
    slots = jnp.arange(NREQ, dtype=jnp.int32)
    matches = slot_of[None, :] == slots[:, None]
    request_at = lax.optimization_barrier(jnp.sum(jnp.where(matches, slots[None, :], 0), axis=1)).astype(jnp.int32)
    starts = jnp.take(cached_len, request_at)
    position = jnp.repeat(starts, CH) + jnp.tile(jnp.arange(CH, dtype=jnp.int32), NREQ)
    query = rotate(normalize(query_raw.reshape(NTOK, NH, HD)) * query_gain, position).astype(jnp.bfloat16)
    keyval = keyval_raw.reshape(NTOK, KVH, 2, HD)
    key = rotate(normalize(keyval[:, :, 0]) * key_gain, position).astype(jnp.bfloat16)
    value = normalize(keyval[:, :, 1]).astype(jnp.bfloat16)
    per_group = NH // KVH
    score_scale = HD ** (-0.5)
    cached_rows = MAXP * PAGE

    def one_slot(slot):
        request = jnp.take(request_at, slot)
        home_group = request // REQ_DEV
        length = jnp.take(cached_len, request)
        pages = home_group * POOL + jnp.take(page_table, request, axis=0)
        stored = jnp.take(cache_pool, pages, axis=0).reshape(cached_rows, KVH, 2, HD)
        begin = (slot * CH).astype(jnp.int32)
        block_queries = lax.dynamic_slice_in_dim(query, begin, CH, 0).astype(jnp.float32)
        fresh_keys = lax.dynamic_slice_in_dim(key, begin, CH, 0)
        fresh_values = lax.dynamic_slice_in_dim(value, begin, CH, 0)
        all_keys = jnp.repeat(jnp.concatenate([stored[:, :, 0], fresh_keys], axis=0), per_group, axis=1)
        all_values = jnp.repeat(jnp.concatenate([stored[:, :, 1], fresh_values], axis=0), per_group, axis=1)
        scores = jnp.einsum('tnh,knh->ntk', block_queries, all_keys.astype(jnp.float32)) * score_scale
        cached_seen = jnp.broadcast_to((jnp.arange(cached_rows) < length)[None, :], (CH, cached_rows))
        causal = jnp.arange(CH)[None, :] <= jnp.arange(CH)[:, None]
        visible = jnp.concatenate([cached_seen, causal], axis=1)[None]
        highest = lax.optimization_barrier(jnp.max(jnp.where(visible, scores, -jnp.inf), axis=-1, keepdims=True))
        expd = jnp.where(visible, jnp.exp(scores - highest), 0.0)
        weights = (expd / lax.optimization_barrier(jnp.sum(expd, axis=-1, keepdims=True))).astype(jnp.bfloat16)
        result = jnp.einsum('ntk,knh->tnh', weights.astype(jnp.float32), all_values.astype(jnp.float32))
        return result.astype(jnp.bfloat16).reshape(CH, NH * HD)
    attended = lax.map(one_slot, slots).reshape(NTOK, NH * HD)
    projected = jnp.dot(attended, w_output, preferred_element_type=jnp.float32)
    attn = normalize(projected) * post_gain
    low = jnp.dot(normed, laurel_left, preferred_element_type=jnp.float32).astype(jnp.bfloat16)
    laurel = normed.astype(jnp.float32) + normalize(jnp.dot(low, laurel_right, preferred_element_type=jnp.float32)) * laurel_gain
    return ((attn + inputs + laurel) / math.sqrt(2.0)).astype(jnp.bfloat16)
```

```python
import functools
import math

import jax
import jax.numpy as jnp
import numpy as np
from jax import lax
from jax.experimental import pallas as pl
from jax.experimental.pallas import tpu as pltpu
from jax.sharding import PartitionSpec as P

NH = 8
KVH = 2
HD = 256
REQ_DEV = 4
CH = 512
EPS = 1e-06
LOG2E = 1.4426950408889634
MASKED = -1e30
VMEM_BYTES = 56 * 1024 * 1024

ANY = pl.BlockSpec(memory_space=pl.ANY)
SMEM = pl.BlockSpec(memory_space=pltpu.SMEM)
VMEM = pl.BlockSpec(memory_space=pltpu.VMEM)


def params(**more):
    return pltpu.CompilerParams(vmem_limit_bytes=VMEM_BYTES, **more)


def rope_table(rows):
    half = HD // 2
    inverse = 1000000.0 ** (-2.0 * np.arange(half) / HD)
    angle = np.arange(rows)[:, None] * inverse[None, :]
    return np.concatenate([np.cos(angle), np.sin(angle)], axis=1).astype(np.float32)


def normalize(values):
    return values * lax.rsqrt(jnp.mean(values * values, axis=-1, keepdims=True) + EPS)


def request_of(slot_of, slot):
    return lax.fori_loop(
        0,
        slot_of.shape[0],
        lambda i, found: jnp.where(slot_of[i] == slot, i, found),
        jnp.int32(0),
    )


def mover_to(slot_of, group, target):
    def step(i, found):
        request = group * REQ_DEV + i
        return jnp.where(slot_of[request] // REQ_DEV == target, request, found)

    return lax.fori_loop(0, REQ_DEV, step, jnp.int32(0))


def pages_kernel(me, slot_of, page_table, pool, near, far, sems):
    group, member = me[0], me[1]
    to_near = mover_to(slot_of, group, me[2])
    to_far = mover_to(slot_of, group, me[3])
    count, part = near.shape[0], far.shape[0]
    copies = []
    for p in range(part):
        page = page_table[to_far, (member % 2) * part + p]
        copies.append(pltpu.make_async_copy(pool.at[page], far.at[p], sems.at[p]))
    for p in range(count):
        page = page_table[to_near, p]
        copies.append(pltpu.make_async_copy(pool.at[page], near.at[p], sems.at[part + p]))
    for copy in copies:
        copy.start()
    for copy in copies:
        copy.wait()


def qkv_kernel(
    me, slot_of, cached_len, tokens, gain, w_query, w_keyval, query_gain, key_gain, table,
    query, key, value, normed, cosine, sine,
):
    step = pl.program_id(0)
    rows = tokens.shape[0]
    per_step = w_query.shape[1] // HD
    query_steps = NH // per_step

    @pl.when(step == 0)
    def _():
        request = request_of(slot_of, me[4])
        start = cached_len[request] + me[5]
        base = table[pl.ds(start, 1), :]
        half = HD // 2
        cos_base, sin_base = base[:, :half], base[:, half:]
        cos_row, sin_row = table[:rows, :half], table[:rows, half:]
        cosine[...] = cos_base * cos_row - sin_base * sin_row
        sine[...] = sin_base * cos_row + cos_base * sin_row
        tile = 64

        def norm_rows(i, _):
            at = pl.ds(pl.multiple_of(i * tile, tile), tile)
            inputs = tokens[at, :].astype(jnp.float32)
            normed[at, :] = (normalize(inputs) * gain[...]).astype(jnp.bfloat16)
            return 0

        lax.fori_loop(0, rows // tile, norm_rows, 0)

    def rotated(raw, head_gain):
        half = HD // 2
        v = normalize(raw) * head_gain[...]
        a, b = v[:, :half], v[:, half:]
        c, s = cosine[...], sine[...]
        return jnp.concatenate([a * c - b * s, b * c + a * s], axis=1).astype(jnp.bfloat16)

    @pl.when(step < query_steps)
    def _():
        for h in range(per_step):
            raw = jnp.dot(
                normed[...], w_query[:, h * HD : (h + 1) * HD], preferred_element_type=jnp.float32
            )
            query[h] = rotated(raw, query_gain)

    @pl.when(step >= query_steps)
    def _():
        raw = jnp.dot(normed[...], w_keyval[:, :HD], preferred_element_type=jnp.float32)
        key[0] = rotated(raw, key_gain)
        raw = jnp.dot(normed[...], w_keyval[:, HD:], preferred_element_type=jnp.float32)
        value[0] = normalize(raw).astype(jnp.bfloat16)


def residual_kernel(tokens, gain, left, right, laurel_gain, out):
    tile = 128
    rows = tokens.shape[0]
    for i in range(rows // tile):
        at = slice(i * tile, (i + 1) * tile)
        inputs = tokens[at, :].astype(jnp.float32)
        normed = (normalize(inputs) * gain[...]).astype(jnp.bfloat16)
        low = jnp.dot(normed, left[...], preferred_element_type=jnp.float32).astype(jnp.bfloat16)
        up = jnp.dot(low, right[...], preferred_element_type=jnp.float32)
        laurel = normed.astype(jnp.float32) + normalize(up) * laurel_gain[...]
        out[at, :] = inputs + laurel


def attention_kernel(
    me, slot_of, cached_len, page_table, query, key, value, pool, near, far_own, far_other,
    out, stored, sems,
):
    kv = pl.program_id(0)
    group, member = me[0], me[1]
    slot = me[4]
    request = request_of(slot_of, slot)
    length = cached_len[request]
    home = request // REQ_DEV
    page_count, page_rows = near.shape[0], near.shape[1]
    cached_rows = page_count * page_rows
    part = page_count // 2
    width = 2 * HD

    @pl.when(kv == 0)
    def _():
        def fetch(source_of):
            for p in range(page_count):
                source = source_of(p)
                for g in range(KVH):
                    pltpu.make_async_copy(
                        source.at[:, g * width : (g + 1) * width],
                        stored.at[g, p * page_rows : (p + 1) * page_rows],
                        sems.at[g, p],
                    ).start()

        @pl.when(home == group)
        def _():
            fetch(lambda p: pool.at[page_table[request, p]])

        @pl.when(home == me[2])
        def _():
            fetch(lambda p: near.at[p])

        @pl.when(home == me[3])
        def _():
            @pl.when(member % 2 == 0)
            def _():
                fetch(lambda p: far_own.at[p] if p < part else far_other.at[p - part])

            @pl.when(member % 2 == 1)
            def _():
                fetch(lambda p: far_other.at[p] if p < part else far_own.at[p - part])

    for p in range(page_count):
        pltpu.make_async_copy(
            near.at[p, :, :width],
            stored.at[kv, p * page_rows : (p + 1) * page_rows],
            sems.at[kv, p],
        ).wait()

    scale = HD ** (-0.5) * LOG2E
    heads, rows = query.shape[0], query.shape[1]
    fresh = key.shape[1]
    tile = 256
    at_key = lax.broadcasted_iota(jnp.int32, (1, cached_rows), 1)
    bias = jnp.where(at_key < length, 0.0, MASKED)
    contract = (((1,), (1,)), ((), ()))

    def one_head(h, _):
        for t in range(rows // tile):
            q = query[h, t * tile : (t + 1) * tile]
            old = lax.dot_general(
                q, stored[kv, :, :HD], contract, preferred_element_type=jnp.float32
            ) * scale + bias
            seen = fresh if fresh > rows else (t + 1) * tile
            new = lax.dot_general(
                q, key[0, :seen], contract, preferred_element_type=jnp.float32
            ) * scale
            row = me[5] + t * tile + lax.broadcasted_iota(jnp.int32, (tile, seen), 0)
            column = lax.broadcasted_iota(jnp.int32, (tile, seen), 1)
            new = jnp.where(column <= row, new, MASKED)
            highest = jnp.maximum(
                jnp.max(old, axis=1, keepdims=True), jnp.max(new, axis=1, keepdims=True)
            )
            old = jnp.exp2(old - highest)
            new = jnp.exp2(new - highest)
            total = jnp.sum(old, axis=1, keepdims=True) + jnp.sum(new, axis=1, keepdims=True)
            result = jnp.dot(
                old.astype(jnp.bfloat16), stored[kv, :, HD:], preferred_element_type=jnp.float32
            ) + jnp.dot(
                new.astype(jnp.bfloat16), value[0, :seen], preferred_element_type=jnp.float32
            )
            out[h, t * tile : (t + 1) * tile] = (result / total).astype(jnp.bfloat16)
        return 0

    lax.fori_loop(0, heads, one_head, 0)


def output_kernel(count, me, attended, residual, post_gain, *rest):
    weights, out = rest[:count], rest[count]
    held, total, sems = rest[count + 1 :]
    copies = [pltpu.make_async_copy(weights[i], held.at[i], sems.at[i]) for i in range(count)]
    for copy in copies:
        copy.start()
    rows = attended.shape[1]
    depth = held.shape[1]
    per_head = HD // depth
    tile = 256
    for i in range(count):
        copies[i].wait()
        block = me[0] ^ i
        head, part = block // per_head, block % per_head
        for t in range(rows // tile):
            at = slice(t * tile, (t + 1) * tile)
            if per_head == 1:
                lhs = attended[head, at]
            else:
                lhs = attended[head, at, pl.ds(pl.multiple_of(part * depth, depth), depth)]
            product = jnp.dot(lhs, held[i], preferred_element_type=jnp.float32)
            if i == 0:
                total[at] = product
            elif i < count - 1:
                total[at] += product
            else:
                projected = total[at] + product
                attn = normalize(projected) * post_gain[...]
                out[at] = ((attn + residual[at]) * (1.0 / math.sqrt(2.0))).astype(jnp.bfloat16)


def shards(
    tokens, input_gain, w_query, w_keyval, query_gain, key_gain, w_output, laurel_left,
    laurel_right, laurel_gain, post_gain, cache_pool, page_table, cached_len, slot_of,
):
    groups = lax.axis_size("req")
    members = lax.axis_size("head")
    group = lax.axis_index("req")
    member = lax.axis_index("head")
    rows, width = tokens.shape
    page_count = page_table.shape[1]
    page_rows = cache_pool.shape[1]
    channels = cache_pool.shape[2]
    share = CH // rows

    near_pairs = [(i, i ^ 1) for i in range(groups)]
    far_pairs = [(i, (i + 1) % groups if i % 2 else (i - 1) % groups) for i in range(groups)]
    far_group = jnp.where(group % 2 == 1, group + 1, group + groups - 1) % groups
    me = jnp.stack(
        [
            group,
            member,
            group ^ 1,
            far_group,
            group * REQ_DEV + member // share,
            member % share * rows,
        ]
    ).astype(jnp.int32)

    part = page_count // 2
    page_shape = (page_rows, channels)
    near_out, far_out = pl.pallas_call(
        pages_kernel,
        out_shape=(
            jax.ShapeDtypeStruct((page_count,) + page_shape, jnp.bfloat16),
            jax.ShapeDtypeStruct((part,) + page_shape, jnp.bfloat16),
        ),
        in_specs=[SMEM, SMEM, SMEM, ANY],
        out_specs=(ANY, ANY),
        scratch_shapes=[pltpu.SemaphoreType.DMA((page_count + part,))],
        compiler_params=params(),
        name="pages",
    )(me, slot_of, page_table, cache_pool)
    far_own = lax.ppermute(far_out, "req", far_pairs)
    near = lax.ppermute(near_out, "req", near_pairs)
    far_other = lax.ppermute(far_own, "head", [(i, i ^ 1) for i in range(members)])

    blocks = {0: w_output}
    for k in range(2, groups, 2):
        blocks[k] = lax.ppermute(w_output, "req", [(i, i ^ k) for i in range(groups)])
    for k in range(0, groups, 2):
        blocks[k + 1] = lax.ppermute(blocks[k], "req", near_pairs)

    gain = input_gain.reshape(1, width)
    table = rope_table(page_count * page_rows + CH)
    per_step = 2
    query_steps = NH // per_step
    whole = lambda shape: pl.BlockSpec(shape, lambda j: (0,) * len(shape))
    query, key, value = pl.pallas_call(
        qkv_kernel,
        grid=(query_steps + KVH,),
        out_shape=(
            jax.ShapeDtypeStruct((NH, rows, HD), jnp.bfloat16),
            jax.ShapeDtypeStruct((KVH, rows, HD), jnp.bfloat16),
            jax.ShapeDtypeStruct((KVH, rows, HD), jnp.bfloat16),
        ),
        in_specs=[
            SMEM,
            SMEM,
            SMEM,
            whole((rows, width)),
            whole((1, width)),
            pl.BlockSpec((width, per_step * HD), lambda j: (0, jnp.minimum(j, query_steps - 1))),
            pl.BlockSpec((width, 2 * HD), lambda j: (0, jnp.maximum(j - query_steps, 0))),
            whole((1, HD)),
            whole((1, HD)),
            whole(table.shape),
        ],
        out_specs=(
            pl.BlockSpec((per_step, rows, HD), lambda j: (jnp.minimum(j, query_steps - 1), 0, 0)),
            pl.BlockSpec((1, rows, HD), lambda j: (jnp.maximum(j - query_steps, 0), 0, 0)),
            pl.BlockSpec((1, rows, HD), lambda j: (jnp.maximum(j - query_steps, 0), 0, 0)),
        ),
        scratch_shapes=[
            pltpu.VMEM((rows, width), jnp.bfloat16),
            pltpu.VMEM((rows, HD // 2), jnp.float32),
            pltpu.VMEM((rows, HD // 2), jnp.float32),
        ],
        compiler_params=params(),
        cost_estimate=pl.CostEstimate(
            flops=2 * rows * width * 3072, bytes_accessed=20 << 20, transcendentals=0
        ),
        name="qkv",
    )(
        me, slot_of, cached_len, tokens, gain, w_query, w_keyval,
        query_gain.reshape(1, HD), key_gain.reshape(1, HD), table,
    )

    residual = pl.pallas_call(
        residual_kernel,
        out_shape=jax.ShapeDtypeStruct((rows, width), jnp.float32),
        in_specs=[VMEM] * 5,
        out_specs=VMEM,
        compiler_params=params(),
        cost_estimate=pl.CostEstimate(
            flops=4 * rows * width * 64, bytes_accessed=6 << 20, transcendentals=0
        ),
        name="residual",
    )(tokens, gain, laurel_left, laurel_right, laurel_gain.reshape(1, width))

    if share > 1:
        team = [list(range(m, m + share)) for m in range(0, members, share)]
        both = lax.all_gather(
            jnp.concatenate([key, value], axis=2), "head", axis=1, tiled=True,
            axis_index_groups=team,
        )
        key, value = both[:, :, :HD], both[:, :, HD:]

    per_kv = NH // KVH
    attended = pl.pallas_call(
        attention_kernel,
        grid=(KVH,),
        out_shape=jax.ShapeDtypeStruct((NH, rows, HD), jnp.bfloat16),
        in_specs=[
            SMEM,
            SMEM,
            SMEM,
            SMEM,
            pl.BlockSpec((per_kv, rows, HD), lambda j: (j, 0, 0)),
            pl.BlockSpec((1, CH, HD), lambda j: (j, 0, 0)),
            pl.BlockSpec((1, CH, HD), lambda j: (j, 0, 0)),
            ANY,
            ANY,
            ANY,
            ANY,
        ],
        out_specs=pl.BlockSpec((per_kv, rows, HD), lambda j: (j, 0, 0)),
        scratch_shapes=[
            pltpu.VMEM((KVH, page_count * page_rows, 2 * HD), jnp.bfloat16),
            pltpu.SemaphoreType.DMA((KVH, page_count)),
        ],
        compiler_params=params(),
        cost_estimate=pl.CostEstimate(
            flops=4 * NH * rows * 1536 * HD, bytes_accessed=8 << 20,
            transcendentals=NH * rows * 1536,
        ),
        name="attention",
    )(
        me, slot_of, cached_len, page_table, query, key, value, cache_pool,
        near, far_own, far_other,
    )

    depth = w_output.shape[0]
    return pl.pallas_call(
        functools.partial(output_kernel, groups),
        out_shape=jax.ShapeDtypeStruct((rows, width), jnp.bfloat16),
        in_specs=[SMEM, VMEM, VMEM, VMEM] + [ANY] * groups,
        out_specs=VMEM,
        scratch_shapes=[
            pltpu.VMEM((groups, depth, width), jnp.bfloat16),
            pltpu.VMEM((rows, width), jnp.float32),
            pltpu.SemaphoreType.DMA((groups,)),
        ],
        compiler_params=params(),
        cost_estimate=pl.CostEstimate(
            flops=2 * rows * width * width, bytes_accessed=16 << 20, transcendentals=0
        ),
        name="project",
    )(me, attended, residual, post_gain.reshape(1, width), *[blocks[k] for k in range(groups)])


def solution(mesh):
    in_specs = (
        P(("req", "head"), None),
        P(),
        P(),
        P(),
        P(),
        P(),
        P("req", None),
        P(),
        P(),
        P(),
        P(),
        P("req", None, None),
        P(),
        P(),
        P(),
    )
    out_specs = P(("req", "head"), None)
    return jax.shard_map(shards, mesh=mesh, in_specs=in_specs, out_specs=out_specs, check_vma=False)
```

```python
import functools
import math

import jax
import jax.numpy as jnp
import numpy as np
from jax import lax
from jax.experimental import pallas as pl
from jax.experimental.pallas import tpu as pltpu
from jax.sharding import PartitionSpec as P

NH = 8
KVH = 2
HD = 256
REQ_DEV = 4
CH = 512
EPS = 1e-06
LOG2E = 1.4426950408889634
MASKED = -1e30
VMEM_BYTES = 63 * 1024 * 1024

SHORT = pl.CostEstimate(flops=1, bytes_accessed=1, transcendentals=0)

ANY = pl.BlockSpec(memory_space=pl.ANY)
SMEM = pl.BlockSpec(memory_space=pltpu.SMEM)
VMEM = pl.BlockSpec(memory_space=pltpu.VMEM)


def params(**more):
    return pltpu.CompilerParams(vmem_limit_bytes=VMEM_BYTES, **more)


def rope_table(rows):
    half = HD // 2
    inverse = 1000000.0 ** (-2.0 * np.arange(half) / HD)
    angle = np.arange(rows)[:, None] * inverse[None, :]
    return np.concatenate([np.cos(angle), np.sin(angle)], axis=1).astype(np.float32)


def normalize(values):
    return values * lax.rsqrt(jnp.mean(values * values, axis=-1, keepdims=True) + EPS)


def request_of(slot_of, slot):
    return lax.fori_loop(
        0,
        slot_of.shape[0],
        lambda i, found: jnp.where(slot_of[i] == slot, i, found),
        jnp.int32(0),
    )


def mover_to(slot_of, group, target):
    def step(i, found):
        request = group * REQ_DEV + i
        return jnp.where(slot_of[request] // REQ_DEV == target, request, found)

    return lax.fori_loop(0, REQ_DEV, step, jnp.int32(0))


def pages_kernel(me, slot_of, page_table, pool, near, *rest):
    fars, (near_held, far_held, sems, out_sems) = rest[:KVH], rest[KVH:]
    member = me[1]
    to_near = mover_to(slot_of, me[0], me[2])
    to_far = mover_to(slot_of, me[0], me[3])
    count, part = near.shape[0], fars[0].shape[0]
    width = 2 * HD
    copies = []
    for p in range(part):
        page = page_table[to_far, (member % 2) * part + p]
        copies.append(pltpu.make_async_copy(pool.at[page], far_held.at[p], sems.at[p]))
    for p in range(count):
        page = page_table[to_near, p]
        copies.append(pltpu.make_async_copy(pool.at[page], near_held.at[p], sems.at[part + p]))
    for copy in copies:
        copy.start()
    moves = []
    for p in range(part):
        copies[p].wait()
        for g in range(KVH):
            move = pltpu.make_async_copy(
                far_held.at[p, :, g * width : (g + 1) * width], fars[g].at[p], out_sems.at[g, p]
            )
            move.start()
            moves.append(move)
    for p in range(count):
        copies[part + p].wait()
        move = pltpu.make_async_copy(near_held.at[p], near.at[p], out_sems.at[KVH, p])
        move.start()
        moves.append(move)
    for move in moves:
        move.wait()


def qkv_kernel(
    me, slot_of, cached_len, tokens, gain, w_query, w_keyval, query_gain, key_gain, table,
    query, key, value, normed, cosine, sine,
):
    step = pl.program_id(0)
    rows = tokens.shape[0]
    per_step = w_query.shape[1] // HD
    query_steps = NH // per_step

    @pl.when(step == 0)
    def _():
        request = request_of(slot_of, me[4])
        start = cached_len[request] + me[5]
        base = table[pl.ds(start, 1), :]
        half = HD // 2
        cos_base, sin_base = base[:, :half], base[:, half:]
        cos_row, sin_row = table[:rows, :half], table[:rows, half:]
        cosine[...] = cos_base * cos_row - sin_base * sin_row
        sine[...] = sin_base * cos_row + cos_base * sin_row
        tile = 64

        def norm_rows(i, _):
            at = pl.ds(pl.multiple_of(i * tile, tile), tile)
            inputs = tokens[at, :].astype(jnp.float32)
            normed[at, :] = (normalize(inputs) * gain[...]).astype(jnp.bfloat16)
            return 0

        lax.fori_loop(0, rows // tile, norm_rows, 0)

    def rotated(raw, head_gain):
        half = HD // 2
        v = normalize(raw) * head_gain[...]
        a, b = v[:, :half], v[:, half:]
        c, s = cosine[...], sine[...]
        return jnp.concatenate([a * c - b * s, b * c + a * s], axis=1).astype(jnp.bfloat16)

    @pl.when(step < query_steps)
    def _():
        for h in range(per_step):
            raw = jnp.dot(
                normed[...], w_query[:, h * HD : (h + 1) * HD], preferred_element_type=jnp.float32
            )
            query[h] = rotated(raw, query_gain)

    @pl.when(step >= query_steps)
    def _():
        raw = jnp.dot(normed[...], w_keyval[:, :HD], preferred_element_type=jnp.float32)
        key[0] = rotated(raw, key_gain)
        raw = jnp.dot(normed[...], w_keyval[:, HD:], preferred_element_type=jnp.float32)
        value[0] = normalize(raw).astype(jnp.bfloat16)


def residual_kernel(tokens, gain, left, right, laurel_gain, out):
    tile = 128
    rows = tokens.shape[0]
    for i in range(rows // tile):
        at = slice(i * tile, (i + 1) * tile)
        inputs = tokens[at, :].astype(jnp.float32)
        normed = (normalize(inputs) * gain[...]).astype(jnp.bfloat16)
        low = lax.dot_general(
            normed, left[...], (((1,), (1,)), ((), ())), preferred_element_type=jnp.float32
        ).astype(jnp.bfloat16)
        up = jnp.dot(low, right[...], preferred_element_type=jnp.float32)
        laurel = normed.astype(jnp.float32) + normalize(up) * laurel_gain[...]
        out[at, :] = inputs + laurel


def attention_kernel(
    kv, me, slot_of, cached_len, page_table, query, key, value, pool, near, far_own, far_other,
    out, stored, sems,
):
    group, member = me[0], me[1]
    request = request_of(slot_of, me[4])
    length = cached_len[request]
    home = request // REQ_DEV
    page_count, page_rows = near.shape[0], near.shape[1]
    cached_rows = page_count * page_rows
    part = page_count // 2
    width = 2 * HD
    channels = slice(kv * width, (kv + 1) * width)

    def copy_page(source, p):
        return pltpu.make_async_copy(
            source, stored.at[pl.ds(p * page_rows, page_rows)], sems.at[p]
        )

    @pl.when(home == group)
    def _():
        for p in range(page_count):
            copy_page(pool.at[page_table[request, p], :, channels], p).start()

    @pl.when(home == me[2])
    def _():
        for p in range(page_count):
            copy_page(near.at[p, :, channels], p).start()

    @pl.when(home == me[3])
    def _():
        own_first = (member % 2) * part
        for p in range(part):
            copy_page(far_own.at[p], own_first + p).start()
            copy_page(far_other.at[p], part - own_first + p).start()

    for p in range(page_count):
        copy_page(near.at[p, :, channels], p).wait()

    scale = HD ** (-0.5) * LOG2E
    heads, rows = query.shape[0], query.shape[1]
    fresh = key.shape[1]
    tile = 256
    at_key = lax.broadcasted_iota(jnp.int32, (1, cached_rows), 1)
    bias = jnp.where(at_key < length, 0.0, MASKED)
    contract = (((1,), (1,)), ((), ()))

    def one_head(h, _):
        for t in range(rows // tile):
            q = query[h, t * tile : (t + 1) * tile]
            old = lax.dot_general(
                q, stored[:, :HD], contract, preferred_element_type=jnp.float32
            ) * scale + bias
            seen = fresh if fresh > rows else (t + 1) * tile
            new = lax.dot_general(
                q, key[0, :seen], contract, preferred_element_type=jnp.float32
            ) * scale
            row = me[5] + t * tile + lax.broadcasted_iota(jnp.int32, (tile, seen), 0)
            column = lax.broadcasted_iota(jnp.int32, (tile, seen), 1)
            new = jnp.where(column <= row, new, MASKED)
            highest = jnp.maximum(
                jnp.max(old, axis=1, keepdims=True), jnp.max(new, axis=1, keepdims=True)
            )
            old = jnp.exp2(old - highest)
            new = jnp.exp2(new - highest)
            total = jnp.sum(old, axis=1, keepdims=True) + jnp.sum(new, axis=1, keepdims=True)
            result = jnp.dot(
                old.astype(jnp.bfloat16), stored[:, HD:], preferred_element_type=jnp.float32
            ) + jnp.dot(
                new.astype(jnp.bfloat16), value[0, :seen], preferred_element_type=jnp.float32
            )
            out[h, t * tile : (t + 1) * tile] = (result / total).astype(jnp.bfloat16)
        return 0

    lax.fori_loop(0, heads, one_head, 0)


def output_kernel(places, me, *refs):
    attended, residual, post_gain = refs[:KVH], refs[KVH], refs[KVH + 1]
    weights, out = refs[KVH + 2 : -5], refs[-5]
    held, heads, total, sems = refs[-4:]
    depth = held.shape[1]
    copies = {}
    for i, (k, offset) in enumerate(places):
        copy = pltpu.make_async_copy(
            weights[i], held.at[k, offset : offset + weights[i].shape[0]], sems.at[i]
        )
        copy.start()
        copies.setdefault(k, []).append(copy)
    per_kv, rows = attended[0].shape[0], attended[0].shape[1]
    for g in range(KVH):
        heads[g * per_kv : (g + 1) * per_kv] = attended[g][...]
    per_head = HD // depth
    tile = 256
    order = list(copies)
    for i, k in enumerate(order):
        for copy in copies[k]:
            copy.wait()
        block = me[0] ^ k
        head, part = block // per_head, block % per_head
        for t in range(rows // tile):
            at = slice(t * tile, (t + 1) * tile)
            if per_head == 1:
                lhs = heads[head, at]
            else:
                lhs = heads[head, at, pl.ds(pl.multiple_of(part * depth, depth), depth)]
            product = jnp.dot(lhs, held[k], preferred_element_type=jnp.float32)
            if i == 0:
                total[at] = product
            elif i < len(order) - 1:
                total[at] += product
            else:
                projected = total[at] + product
                attn = normalize(projected) * post_gain[...]
                out[at] = ((attn + residual[at]) * (1.0 / math.sqrt(2.0))).astype(jnp.bfloat16)


def shards(
    tokens, input_gain, w_query, w_keyval, query_gain, key_gain, w_output, laurel_left,
    laurel_right, laurel_gain, post_gain, cache_pool, page_table, cached_len, slot_of,
):
    groups = lax.axis_size("req")
    members = lax.axis_size("head")
    group = lax.axis_index("req")
    member = lax.axis_index("head")
    rows, width = tokens.shape
    page_count = page_table.shape[1]
    page_rows = cache_pool.shape[1]
    channels = cache_pool.shape[2]
    share = CH // rows

    near_pairs = [(i, i ^ 1) for i in range(groups)]
    far_pairs = [(i, (i + 1) % groups if i % 2 else (i - 1) % groups) for i in range(groups)]
    far_group = jnp.where(group % 2 == 1, group + 1, group + groups - 1) % groups
    me = jnp.stack(
        [
            group,
            member,
            group ^ 1,
            far_group,
            group * REQ_DEV + member // share,
            member % share * rows,
        ]
    ).astype(jnp.int32)

    part = page_count // 2
    near_shape = (page_count, page_rows, channels)
    far_shape = (part, page_rows, 2 * HD)
    near_out, *far_out = pl.pallas_call(
        pages_kernel,
        out_shape=(jax.ShapeDtypeStruct(near_shape, jnp.bfloat16),)
        + (jax.ShapeDtypeStruct(far_shape, jnp.bfloat16),) * KVH,
        in_specs=[SMEM, SMEM, SMEM, ANY],
        out_specs=(ANY,) * (1 + KVH),
        scratch_shapes=[
            pltpu.VMEM(near_shape, jnp.bfloat16),
            pltpu.VMEM((part, page_rows, channels), jnp.bfloat16),
            pltpu.SemaphoreType.DMA((page_count + part,)),
            pltpu.SemaphoreType.DMA((KVH + 1, page_count)),
        ],
        compiler_params=params(),
        name="pages",
    )(me, slot_of, page_table, cache_pool)

    def send(block, axis, pairs):
        return lax.ppermute(block, axis, pairs)

    def flip(k):
        return [(i, i ^ k) for i in range(groups)]

    def after(block, *others):
        return lax.optimization_barrier((block,) + others)[0]

    side = [(i, i ^ 1) for i in range(members)]
    far_hop = groups // 2
    across = send(w_output, "req", flip(far_hop))
    half = w_output.shape[0] // 2
    halves = [w_output[:half], w_output[half:]]
    hops = range(2, far_hop, 2)
    first = {k: send(halves[0], "req", flip(k)) for k in hops}
    far_own = [send(far, "req", far_pairs) for far in far_out]
    near = send(near_out, "req", near_pairs)

    gain = input_gain.reshape(1, width)
    table = rope_table(page_count * page_rows + CH)
    per_step = 2
    query_steps = NH // per_step
    whole = lambda shape: pl.BlockSpec(shape, lambda j: (0,) * len(shape))
    query, key, value = pl.pallas_call(
        qkv_kernel,
        grid=(query_steps + KVH,),
        out_shape=(
            jax.ShapeDtypeStruct((NH, rows, HD), jnp.bfloat16),
            jax.ShapeDtypeStruct((KVH, rows, HD), jnp.bfloat16),
            jax.ShapeDtypeStruct((KVH, rows, HD), jnp.bfloat16),
        ),
        in_specs=[
            SMEM,
            SMEM,
            SMEM,
            whole((rows, width)),
            whole((1, width)),
            pl.BlockSpec((width, per_step * HD), lambda j: (0, jnp.minimum(j, query_steps - 1))),
            pl.BlockSpec((width, 2 * HD), lambda j: (0, jnp.maximum(j - query_steps, 0))),
            whole((1, HD)),
            whole((1, HD)),
            whole(table.shape),
        ],
        out_specs=(
            pl.BlockSpec((per_step, rows, HD), lambda j: (jnp.minimum(j, query_steps - 1), 0, 0)),
            pl.BlockSpec((1, rows, HD), lambda j: (jnp.maximum(j - query_steps, 0), 0, 0)),
            pl.BlockSpec((1, rows, HD), lambda j: (jnp.maximum(j - query_steps, 0), 0, 0)),
        ),
        scratch_shapes=[
            pltpu.VMEM((rows, width), jnp.bfloat16),
            pltpu.VMEM((rows, HD // 2), jnp.float32),
            pltpu.VMEM((rows, HD // 2), jnp.float32),
        ],
        compiler_params=params(),
        cost_estimate=SHORT,
        name="qkv",
    )(
        me, slot_of, cached_len, tokens, gain, w_query, w_keyval,
        query_gain.reshape(1, HD), key_gain.reshape(1, HD), table,
    )

    far_other = [None] * KVH
    far_other[0] = send(after(far_own[0], query), "head", side)
    tokens_later = after(tokens, far_own[0], query)

    residual = pl.pallas_call(
        residual_kernel,
        out_shape=jax.ShapeDtypeStruct((rows, width), jnp.float32),
        in_specs=[VMEM] * 5,
        out_specs=VMEM,
        compiler_params=params(),
        cost_estimate=SHORT,
        name="residual",
    )(tokens_later, gain, laurel_left.T, laurel_right, laurel_gain.reshape(1, width))

    far_other[1] = send(after(far_own[1], residual), "head", side)
    pieces = [(0, 0, w_output), (far_hop, 0, across)]
    pieces += [(k + 1, 0, send(after(w, residual), "req", near_pairs)) for k, _, w in pieces]
    rest = after(halves[1], residual, far_own[1])
    second = {k: send(rest, "req", flip(k)) for k in hops}
    relays = {}
    for k in hops:
        block = after(first[k], residual)
        relays[k] = send(block, "req", flip(far_hop))
        pieces += [(k, 0, block), (k + 1, 0, send(block, "req", near_pairs))]
        pieces += [(k + far_hop, 0, relays[k])]

    if share > 1:
        team = [list(range(m, m + share)) for m in range(0, members, share)]
        both = lax.all_gather(
            jnp.concatenate([key, value], axis=2), "head", axis=1, tiled=True,
            axis_index_groups=team,
        )
        key, value = both[:, :, :HD], both[:, :, HD:]

    per_kv = NH // KVH
    def attend(g):
        return pl.pallas_call(
            functools.partial(attention_kernel, g),
            grid=(1,),
            out_shape=jax.ShapeDtypeStruct((per_kv, rows, HD), jnp.bfloat16),
            in_specs=[
                SMEM,
                SMEM,
                SMEM,
                SMEM,
                pl.BlockSpec((per_kv, rows, HD), lambda j: (g, 0, 0)),
                pl.BlockSpec((1, CH, HD), lambda j: (g, 0, 0)),
                pl.BlockSpec((1, CH, HD), lambda j: (g, 0, 0)),
                ANY,
                ANY,
                ANY,
                ANY,
            ],
            out_specs=pl.BlockSpec((per_kv, rows, HD), lambda j: (0, 0, 0)),
            scratch_shapes=[
                pltpu.VMEM((page_count * page_rows, 2 * HD), jnp.bfloat16),
                pltpu.SemaphoreType.DMA((page_count,)),
            ],
            compiler_params=params(),
            cost_estimate=SHORT,
            name="attention",
        )(
            me, slot_of, cached_len, page_table, query, key, value, cache_pool,
            near, far_own[g], far_other[g],
        )

    attended = [attend(0)]
    late = []
    for k in hops:
        block = after(second[k], attended[0])
        relayed = send(block, "req", flip(far_hop))
        early = after(relays[k], attended[0])
        pieces += [(k + far_hop + 1, 0, send(early, "req", near_pairs))]
        pieces += [(k, half, block), (k + 1, half, send(block, "req", near_pairs))]
        late.append((k, relayed))
    attended += [attend(g) for g in range(1, KVH)]
    for k, relayed in late:
        relayed = after(relayed, attended[-1])
        pieces += [(k + far_hop, half, relayed)]
        pieces += [(k + far_hop + 1, half, send(relayed, "req", near_pairs))]

    places = [(k, offset) for k, offset, _ in pieces]
    weights = [w for _, _, w in pieces]
    return pl.pallas_call(
        functools.partial(output_kernel, places),
        out_shape=jax.ShapeDtypeStruct((rows, width), jnp.bfloat16),
        in_specs=[SMEM] + [VMEM] * (KVH + 2) + [ANY] * len(pieces),
        out_specs=VMEM,
        scratch_shapes=[
            pltpu.VMEM((groups, w_output.shape[0], width), jnp.bfloat16),
            pltpu.VMEM((NH, rows, HD), jnp.bfloat16),
            pltpu.VMEM((rows, width), jnp.float32),
            pltpu.SemaphoreType.DMA((len(pieces),)),
        ],
        compiler_params=params(),
        cost_estimate=SHORT,
        name="project",
    )(me, *attended, residual, post_gain.reshape(1, width), *weights)


def solution(mesh):
    in_specs = (
        P(("req", "head"), None),
        P(),
        P(),
        P(),
        P(),
        P(),
        P("req", None),
        P(),
        P(),
        P(),
        P(),
        P("req", None, None),
        P(),
        P(),
        P(),
    )
    out_specs = P(("req", "head"), None)
    return jax.shard_map(shards, mesh=mesh, in_specs=in_specs, out_specs=out_specs, check_vma=False)
```

```python
import functools
import math

import jax
import jax.numpy as jnp
import numpy as np
from jax import lax
from jax.experimental import pallas as pl
from jax.experimental.pallas import tpu as pltpu
from jax.sharding import PartitionSpec as P

NH = 8
KVH = 2
HD = 256
REQ_DEV = 4
CH = 512
EPS = 1e-06
LOG2E = 1.4426950408889634
MASKED = -1e30
VMEM_BYTES = 64 * 1024 * 1024

SHORT = pl.CostEstimate(flops=1, bytes_accessed=1, transcendentals=0)

ANY = pl.BlockSpec(memory_space=pl.ANY)
SMEM = pl.BlockSpec(memory_space=pltpu.SMEM)
VMEM = pl.BlockSpec(memory_space=pltpu.VMEM)


def params(**more):
    return pltpu.CompilerParams(vmem_limit_bytes=VMEM_BYTES, **more)


def rope_table(rows):
    half = HD // 2
    inverse = 1000000.0 ** (-2.0 * np.arange(half) / HD)
    angle = np.arange(rows)[:, None] * inverse[None, :]
    return np.concatenate([np.cos(angle), np.sin(angle)], axis=1).astype(np.float32)


def place():
    groups = lax.axis_size("req")
    group = lax.axis_index("req").astype(jnp.int32)
    member = lax.axis_index("head").astype(jnp.int32)
    odd = group % 2
    near = group + 1 - 2 * odd
    far = lax.rem(group + 2 * odd - 1 + groups, jnp.int32(groups))
    return group, member, near, far


def slot_here(rows):
    share = CH // rows
    group, member, _, _ = place()
    return group * REQ_DEV + member // share, member % share * rows


def normalize(values):
    return values * lax.rsqrt(jnp.mean(values * values, axis=-1, keepdims=True) + EPS)


def request_of(slot_of, slot):
    return lax.fori_loop(
        0,
        slot_of.shape[0],
        lambda i, found: jnp.where(slot_of[i] == slot, i, found),
        jnp.int32(0),
    )


def mover_to(slot_of, group, target):
    def step(i, found):
        request = group * REQ_DEV + i
        return jnp.where(slot_of[request] // REQ_DEV == target, request, found)

    return lax.fori_loop(0, REQ_DEV, step, jnp.int32(0))


def pages_kernel(slot_of, page_table_in, pool, w_output, near, *rest):
    fars, pieces_out = rest[:KVH], rest[KVH : KVH + 2]
    page_table, near_held, far_held, middle, last, sems, in_sems, out_sems = rest[KVH + 2 :]
    table_copy = pltpu.make_async_copy(page_table_in, page_table, in_sems.at[0])
    table_copy.start()
    quarter = last.shape[0]
    pieces = [
        pltpu.make_async_copy(w_output.at[pl.ds(quarter, 2 * quarter)], middle, in_sems.at[1]),
        pltpu.make_async_copy(w_output.at[pl.ds(3 * quarter, quarter)], last, in_sems.at[2]),
    ]
    group, member, near_group, far_group = place()
    to_near = mover_to(slot_of, group, near_group)
    to_far = mover_to(slot_of, group, far_group)
    count, part = near.shape[0], fars[0].shape[0]
    width = 2 * HD
    table_copy.wait()
    copies = []
    for p in range(part):
        page = page_table[(member % 2) * part + p, to_far]
        copies.append(pltpu.make_async_copy(pool.at[page], far_held.at[p], sems.at[p]))
    for p in range(count):
        page = page_table[p, to_near]
        copies.append(pltpu.make_async_copy(pool.at[page], near_held.at[p], sems.at[part + p]))
    for copy in copies + pieces:
        copy.start()
    moves = []
    for p in range(part):
        copies[p].wait()
        for g in range(KVH):
            source = far_held.at[p, :, g * width : (g + 1) * width]
            moves.append(pltpu.make_async_copy(source, fars[g].at[p], out_sems.at[g, p]))
            moves[-1].start()
    for p in range(count):
        copies[part + p].wait()
        moves.append(pltpu.make_async_copy(near_held.at[p], near.at[p], out_sems.at[KVH, p]))
        moves[-1].start()
    for i, (held, out) in enumerate(zip((middle, last), pieces_out)):
        pieces[i].wait()
        moves.append(pltpu.make_async_copy(held, out, in_sems.at[1 + i]))
        moves[-1].start()
    for move in moves:
        move.wait()


def residual_kernel(gain, left, right, laurel_gain, tokens_in, out, tokens, residual, sems, out_sems):
    rows = tokens.shape[0]
    tile = 128
    tiles = rows // tile
    inputs, moves = [], []
    for i in range(tiles):
        at = slice(i * tile, (i + 1) * tile)
        inputs.append(pltpu.make_async_copy(tokens_in.at[at], tokens.at[at], sems.at[i]))
        inputs[i].start()
    for i in range(tiles):
        inputs[i].wait()
        at = slice(i * tile, (i + 1) * tile)
        x = tokens[at, :].astype(jnp.float32)
        normed = (normalize(x) * gain[...]).astype(jnp.bfloat16)
        low = lax.dot_general(
            normed, left[...], (((1,), (1,)), ((), ())), preferred_element_type=jnp.float32
        ).astype(jnp.bfloat16)
        up = jnp.dot(low, right[...], preferred_element_type=jnp.float32)
        laurel = normed.astype(jnp.float32) + normalize(up) * laurel_gain[...]
        residual[at, :] = x + laurel
        moves.append(pltpu.make_async_copy(residual.at[at], out.at[at], out_sems.at[i]))
        moves[i].start()
    for move in moves:
        move.wait()


def qkv_kernel(
    slot_of, cached_len, gain, query_gain, key_gain, tokens_in, w_query_in, w_keyval_in,
    table_in, query_out, key_out, value_out,
    tokens, w_query, w_keyval, table, table_row, normed, cosine, sine, query, key, value,
    in_sems, w_sems, out_sems,
):
    rows = tokens.shape[0]
    half = HD // 2
    chunk = min(128, rows)
    chunks = rows // chunk
    wide = 4 * HD
    tokens_copies = []
    for i in range(chunks):
        at = slice(i * chunk, (i + 1) * chunk)
        copy = pltpu.make_async_copy(tokens_in.at[at], tokens.at[at], in_sems.at[i])
        copy.start()
        tokens_copies.append(copy)
    units = [(0, c) for c in range(0, NH * HD // 2, wide)]
    units += [(1, c) for c in range(0, 2 * KVH * HD, wide)]
    units += [(0, c) for c in range(NH * HD // 2, NH * HD, wide)]
    w_copies = []
    for i, (which, c) in enumerate(units):
        source, held = ((w_query_in, w_query), (w_keyval_in, w_keyval))[which]
        columns = slice(c, c + wide)
        w_copies.append(
            pltpu.make_async_copy(source.at[:, columns], held.at[:, columns], w_sems.at[i])
        )
    w_copies[0].start()
    slot, first_row = slot_here(rows)
    start = cached_len[request_of(slot_of, slot)] + first_row
    aligned = pl.multiple_of(start // 8 * 8, 8)
    row_copy = pltpu.make_async_copy(
        table_in.at[pl.ds(aligned, 8)], table_row, in_sems.at[chunks]
    )
    row_copy.start()
    table_copy = pltpu.make_async_copy(
        table_in.at[pl.ds(0, rows)], table, in_sems.at[chunks + 1]
    )
    tile = 64
    for i in range(rows // tile):
        if i * tile % chunk == 0:
            tokens_copies[i * tile // chunk].wait()
            if i == 0:
                table_copy.start()
                w_copies[1].start()
        at = slice(i * tile, (i + 1) * tile)
        inputs = tokens[at, :].astype(jnp.float32)
        normed[at, :] = (normalize(inputs) * gain[...]).astype(jnp.bfloat16)
    row_copy.wait()
    table_copy.wait()
    base = table_row[pl.ds(start - aligned, 1), :]
    cos_base, sin_base = base[:, :half], base[:, half:]
    cos_row, sin_row = table[:, :half], table[:, half:]
    cosine[...] = cos_base * cos_row - sin_base * sin_row
    sine[...] = sin_base * cos_row + cos_base * sin_row

    sent = []
    tile = 256

    def finish(which, head, t, raw):
        at = slice(t * tile, (t + 1) * tile)
        if which == 1 and head % 2 == 1:
            held, out, place = value, value_out, head // 2
            value[place, at] = normalize(raw).astype(jnp.bfloat16)
        else:
            held, out, place = (query, query_out, head) if which == 0 else (key, key_out, head // 2)
            v = normalize(raw) * (query_gain, key_gain)[which][...]
            x, y = v[:, :half], v[:, half:]
            c, s = cosine[at], sine[at]
            held[place, at, :half] = (x * c - y * s).astype(jnp.bfloat16)
            held[place, at, half:] = (y * c + x * s).astype(jnp.bfloat16)
        if t == rows // tile - 1:
            copy = pltpu.make_async_copy(held.at[place], out.at[place], out_sems.at[len(sent)])
            copy.start()
            sent.append(copy)

    waiting = None
    for i, (which, first) in enumerate(units):
        w_copies[i].wait()
        if i + 2 < len(units):
            w_copies[i + 2].start()
        held = (w_query, w_keyval)[which]
        for c in range(first, first + wide, HD):
            for t in range(rows // tile):
                raw = jnp.dot(
                    normed[t * tile : (t + 1) * tile],
                    held[:, c : c + HD],
                    preferred_element_type=jnp.float32,
                )
                if waiting is not None:
                    finish(*waiting)
                waiting = (which, c // HD, t, raw)
    finish(*waiting)
    for copy in sent:
        copy.wait()


def attention_kernel(
    kv, slot_of, cached_len, page_table_in, query_in, key_in, value_in, pool, near, far_own,
    far_other, *rest,
):
    out_in, (page_table, query, key, value, out, stored, sems, in_sems, out_sems) = (
        rest[-10],
        rest[-9:],
    )
    group, member, near_group, far_group = place()
    table_copy = pltpu.make_async_copy(page_table_in, page_table, in_sems.at[3])
    table_copy.start()
    per_kv, rows = query.shape[0], query.shape[1]
    inputs = [
        pltpu.make_async_copy(query_in.at[pl.ds(kv * per_kv, per_kv)], query, in_sems.at[0]),
        pltpu.make_async_copy(key_in.at[kv], key, in_sems.at[1]),
        pltpu.make_async_copy(value_in.at[kv], value, in_sems.at[2]),
    ]
    for copy in inputs:
        copy.start()
    slot, first_row = slot_here(rows)
    request = request_of(slot_of, slot)
    length = cached_len[request]
    home = request // REQ_DEV
    page_count, page_rows = near.shape[0], near.shape[1]
    cached_rows = page_count * page_rows
    part = page_count // 2
    width = 2 * HD
    channels = slice(kv * width, (kv + 1) * width)

    def copy_page(source, p):
        return pltpu.make_async_copy(
            source, stored.at[pl.ds(p * page_rows, page_rows)], sems.at[p]
        )

    table_copy.wait()

    @pl.when(home == group)
    def _():
        for p in range(page_count):
            copy_page(pool.at[page_table[p, request], :, channels], p).start()

    @pl.when(home == near_group)
    def _():
        for p in range(page_count):
            copy_page(near.at[p, :, channels], p).start()

    @pl.when(home == far_group)
    def _():
        own_first = (member % 2) * part
        for p in range(part):
            copy_page(far_own.at[p], own_first + p).start()
            copy_page(far_other.at[p], part - own_first + p).start()

    for copy in inputs:
        copy.wait()
    for p in range(page_count):
        copy_page(near.at[p, :, channels], p).wait()

    scale = HD ** (-0.5) * LOG2E
    fresh = key.shape[0]
    tile = 256
    at_key = lax.broadcasted_iota(jnp.int32, (1, cached_rows), 1)
    bias = jnp.where(at_key < length, 0.0, MASKED)
    contract = (((1,), (1,)), ((), ()))

    def scores(h, t):
        q = query[h, t * tile : (t + 1) * tile]
        seen = fresh if fresh > rows else (t + 1) * tile
        old = lax.dot_general(q, stored[:, :HD], contract, preferred_element_type=jnp.float32)
        new = lax.dot_general(q, key[:seen], contract, preferred_element_type=jnp.float32)
        return old, new

    def finish(h, t, old, new):
        seen = new.shape[1]
        clear = 0 if fresh > rows else t * tile
        old = old + bias
        row = first_row + t * tile + lax.broadcasted_iota(jnp.int32, (tile, seen - clear), 0)
        column = clear + lax.broadcasted_iota(jnp.int32, (tile, seen - clear), 1)
        edge = jnp.where(column <= row, new[:, clear:], MASKED)
        parts = [(old, stored[:, HD:]), (edge, value[clear:seen])]
        if clear:
            parts.append((new[:, :clear], value[:clear]))
        highest = functools.reduce(
            jnp.maximum, [jnp.max(x, axis=1, keepdims=True) for x, _ in parts]
        )
        parts = [(jnp.exp2((x - highest) * scale), v) for x, v in parts]
        total = functools.reduce(jnp.add, [jnp.sum(x, axis=1, keepdims=True) for x, _ in parts])
        result = functools.reduce(
            jnp.add,
            [
                jnp.dot(x.astype(jnp.bfloat16), v, preferred_element_type=jnp.float32)
                for x, v in parts
            ],
        )
        out[h, t * tile : (t + 1) * tile] = (result / total).astype(jnp.bfloat16)

    def send(h):
        return pltpu.make_async_copy(out.at[h], out_in.at[kv * per_kv + h], out_sems.at[h])

    items = [(h, t) for h in range(per_kv) for t in range(rows // tile)]
    current = scores(*items[0])
    for i, (h, t) in enumerate(items):
        following = scores(*items[i + 1]) if i + 1 < len(items) else None
        finish(h, t, *current)
        current = following
        if t == rows // tile - 1:
            send(h).start()
    for h in range(per_kv):
        send(h).wait()


def output_kernel(places, post_gain, attended, residual_in, *refs):
    arrays = 1 + max(i for _, _, i, _, _ in places)
    weights, out = refs[:arrays], refs[arrays]
    lhs, held, total, residual, result, sems, lhs_sems, res_sems, out_sems = refs[-9:]
    rows, width = total.shape
    depth = refs[0].shape[0]
    per_head = HD // depth
    order = list(dict.fromkeys(k for k, *_ in places))
    wide = 512
    group = place()[0]
    lhs_copies = []
    for i, k in enumerate(order):
        block = group ^ k
        head = block // per_head
        source = attended.at[head]
        if per_head > 1:
            part = pl.multiple_of(block % per_head * depth, depth)
            source = attended.at[head, :, pl.ds(part, depth)]
        copy = pltpu.make_async_copy(
            source, lhs.at[:, i * depth : (i + 1) * depth], lhs_sems.at[i]
        )
        copy.start()
        lhs_copies.append(copy)
    copies = []
    for n in range(width // wide):
        columns = slice(n * wide, (n + 1) * wide)
        copies.append([])
        for p, (k, offset, i, row, count) in enumerate(places):
            first = order.index(k) * depth + offset
            copies[n].append(
                pltpu.make_async_copy(
                    weights[i].at[row : row + count, columns],
                    held.at[first : first + count, columns],
                    sems.at[n, p],
                )
            )
    tile = 128
    res_copies = []
    for t in range(rows // tile):
        at = slice(t * tile, (t + 1) * tile)
        res_copies.append(
            pltpu.make_async_copy(residual_in.at[at], residual.at[at], res_sems.at[t])
        )
    for copy in copies[0] + copies[1]:
        copy.start()
    for copy in lhs_copies:
        copy.wait()
    squares = 0.0
    for n in range(width // wide):
        columns = slice(n * wide, (n + 1) * wide)
        for copy in copies[n]:
            copy.wait()
        for copy in copies[n + 2] if n + 2 < len(copies) else res_copies if n + 2 == len(copies) else []:
            copy.start()
        product = jnp.dot(lhs[...], held[:, columns], preferred_element_type=jnp.float32)
        total[:, columns] = product
        squares += jnp.sum(product * product, axis=1, keepdims=True)
    ratio = lax.rsqrt(squares * (1.0 / width) + EPS)
    out_copies = []
    for t in range(rows // tile):
        at = slice(t * tile, (t + 1) * tile)
        res_copies[t].wait()
        attn = total[at] * ratio[at] * post_gain[...]
        result[at] = ((attn + residual[at]) * (1.0 / math.sqrt(2.0))).astype(jnp.bfloat16)
        copy = pltpu.make_async_copy(result.at[at], out.at[at], out_sems.at[t])
        copy.start()
        out_copies.append(copy)
    for copy in out_copies:
        copy.wait()


def shards(
    tokens, input_gain, w_query, w_keyval, query_gain, key_gain, w_output, laurel_left,
    laurel_right, laurel_gain, post_gain, cache_pool, page_table, cached_len, slot_of,
):
    groups = lax.axis_size("req")
    members = lax.axis_size("head")
    rows, width = tokens.shape
    page_count = page_table.shape[1]
    page_rows = cache_pool.shape[1]
    channels = cache_pool.shape[2]
    share = CH // rows

    near_pairs = [(i, i ^ 1) for i in range(groups)]
    far_pairs = [(i, (i + 1) % groups if i % 2 else (i - 1) % groups) for i in range(groups)]
    def send(block, axis, pairs):
        return lax.ppermute(block, axis, pairs)

    def flip(k):
        return [(i, i ^ k) for i in range(groups)]

    def after(block, *others):
        return lax.optimization_barrier((block,) + others)[0]

    side = [(i, i ^ 1) for i in range(members)]
    far_hop = groups // 2
    top = w_output[: w_output.shape[0] // 4]
    hops = range(2, far_hop, 2)
    side = [(i, i ^ 1) for i in range(members)]
    first = {k: send(top, "req", flip(k)) for k in hops}
    first[far_hop] = send(top, "req", flip(far_hop))
    own_near = send(w_output, "req", near_pairs)
    early_done = [*first.values(), own_near]
    pages_of = page_table.T
    part = page_count // 2
    near_shape = (page_count, page_rows, channels)
    far_shape = (part, page_rows, 2 * HD)
    gain = input_gain.reshape(1, width)
    quarter = w_output.shape[0] // 4
    piece = lambda n: (n * quarter, width)
    near_out, *far_out, middle, last = pl.pallas_call(
        pages_kernel,
        out_shape=(jax.ShapeDtypeStruct(near_shape, jnp.bfloat16),)
        + (jax.ShapeDtypeStruct(far_shape, jnp.bfloat16),) * KVH
        + tuple(jax.ShapeDtypeStruct(piece(n), jnp.bfloat16) for n in (2, 1)),
        in_specs=[SMEM, ANY, ANY, ANY],
        out_specs=(ANY,) * (3 + KVH),
        scratch_shapes=[
            pltpu.SMEM(pages_of.shape, jnp.int32),
            pltpu.VMEM(near_shape, jnp.bfloat16),
            pltpu.VMEM((part, page_rows, channels), jnp.bfloat16),
            pltpu.VMEM(piece(2), jnp.bfloat16),
            pltpu.VMEM(piece(1), jnp.bfloat16),
            pltpu.SemaphoreType.DMA((page_count + part,)),
            pltpu.SemaphoreType.DMA((3,)),
            pltpu.SemaphoreType.DMA((KVH + 1, page_count)),
        ],
        compiler_params=params(),
        cost_estimate=SHORT,
        name="pages",
    )(after(slot_of, top), pages_of, cache_pool, w_output)
    near = send(after(near_out, *early_done), "req", near_pairs)

    far_out = [after(far, *early_done) for far in far_out]
    far_own = [send(far, "req", far_pairs) for far in far_out]
    middle, last = (after(w, *early_done) for w in (middle, last))
    middles = {far_hop: send(middle, "req", flip(far_hop))}
    lasts = {far_hop: send(last, "req", flip(far_hop))}
    relays = {k: send(after(first[k], *early_done), "req", flip(far_hop)) for k in hops}

    table = rope_table(page_count * page_rows + CH)
    heads_shape = lambda heads: jax.ShapeDtypeStruct((heads, rows, HD), jnp.bfloat16)
    query, key, value = pl.pallas_call(
        qkv_kernel,
        out_shape=(heads_shape(NH), heads_shape(KVH), heads_shape(KVH)),
        in_specs=[SMEM, SMEM, VMEM, VMEM, VMEM, ANY, ANY, ANY, ANY],
        out_specs=(ANY,) * 3,
        scratch_shapes=[
            pltpu.VMEM((rows, width), jnp.bfloat16),
            pltpu.VMEM(w_query.shape, jnp.bfloat16),
            pltpu.VMEM(w_keyval.shape, jnp.bfloat16),
            pltpu.VMEM((rows, HD), jnp.float32),
            pltpu.VMEM((8, HD), jnp.float32),
            pltpu.VMEM((rows, width), jnp.bfloat16),
            pltpu.VMEM((rows, HD // 2), jnp.float32),
            pltpu.VMEM((rows, HD // 2), jnp.float32),
            pltpu.VMEM((NH, rows, HD), jnp.bfloat16),
            pltpu.VMEM((KVH, rows, HD), jnp.bfloat16),
            pltpu.VMEM((KVH, rows, HD), jnp.bfloat16),
            pltpu.SemaphoreType.DMA((8,)),
            pltpu.SemaphoreType.DMA((8,)),
            pltpu.SemaphoreType.DMA((NH + 2 * KVH,)),
        ],
        compiler_params=params(),
        cost_estimate=SHORT,
        name="qkv",
    )(
        slot_of, cached_len, gain, query_gain.reshape(1, HD),
        key_gain.reshape(1, HD), tokens, w_query, w_keyval, table,
    )

    far_other = [send(after(far_own[0], query), "head", side)]
    residual = pl.pallas_call(
        residual_kernel,
        out_shape=jax.ShapeDtypeStruct((rows, width), jnp.float32),
        in_specs=[VMEM] * 4 + [ANY],
        out_specs=ANY,
        scratch_shapes=[
            pltpu.VMEM((rows, width), jnp.bfloat16),
            pltpu.VMEM((rows, width), jnp.float32),
            pltpu.SemaphoreType.DMA((4,)),
            pltpu.SemaphoreType.DMA((4,)),
        ],
        compiler_params=params(),
        cost_estimate=SHORT,
        name="residual",
    )(
        gain, laurel_left.T, laurel_right, laurel_gain.reshape(1, width),
        after(tokens, far_own[0], query, near, *relays.values()),
    )
    pieces = [(0, 0, w_output), (1, 0, own_near)]
    shared = []
    for k, block in first.items():
        shared.append(send(after(block, query), "req", near_pairs))
        pieces += [(k, 0, block), (k + 1, 0, shared[-1])]
    far_other += [send(after(far, residual), "head", side) for far in far_own[1:]]
    for k in hops:
        middles[k] = send(after(middle, residual, *far_own), "req", flip(k))

    if share > 1:
        team = [list(range(m, m + share)) for m in range(0, members, share)]
        both = lax.all_gather(
            jnp.concatenate([key, value], axis=2), "head", axis=1, tiled=True,
            axis_index_groups=team,
        )
        key, value = both[:, :, :HD], both[:, :, HD:]

    per_kv = NH // KVH
    def attend(g, earlier=None):
        more = [] if earlier is None else [earlier]
        return pl.pallas_call(
            functools.partial(attention_kernel, g),
            out_shape=heads_shape(NH),
            in_specs=[SMEM] * 2 + [ANY] * (8 + len(more)),
            out_specs=ANY,
            scratch_shapes=[
                pltpu.SMEM(pages_of.shape, jnp.int32),
                pltpu.VMEM((per_kv, rows, HD), jnp.bfloat16),
                pltpu.VMEM((CH, HD), jnp.bfloat16),
                pltpu.VMEM((CH, HD), jnp.bfloat16),
                pltpu.VMEM((per_kv, rows, HD), jnp.bfloat16),
                pltpu.VMEM((page_count * page_rows, 2 * HD), jnp.bfloat16),
                pltpu.SemaphoreType.DMA((page_count,)),
                pltpu.SemaphoreType.DMA((4,)),
                pltpu.SemaphoreType.DMA((per_kv,)),
            ],
            input_output_aliases={10: 0} if more else {},
            compiler_params=params(),
            cost_estimate=SHORT,
            name="attention",
        )(
            slot_of, cached_len, pages_of, query, key, value, cache_pool,
            near, far_own[g], far_other[g], *more,
        )

    attended = [attend(0)]
    late = []
    ahead = after(attended[0], *far_other[1:], *middles.values())
    swapped = []

    def both_cores(k, offset, block):
        swapped.append(send(block, "req", near_pairs))
        if isinstance(k, tuple):
            pieces.append((k, offset, block))
            pieces.append((tuple(j + 1 for j in k), offset, swapped[-1]))
        else:
            pieces.extend([(k, offset, block), (k + 1, offset, swapped[-1])])

    for k in hops:
        here = after(middles[k], ahead)
        both_cores(k, quarter, here)
        both_cores(k + far_hop, 0, after(relays[k], ahead))
        late.append((k + far_hop, quarter, send(here, "req", flip(far_hop))))
        here = after(lasts[far_hop], ahead)
        both = send(jnp.concatenate([after(last, ahead), here], axis=0), "req", flip(k))
        late.append(((k, k + far_hop), 3 * quarter, both))
    for offset, block in ((quarter, middles[far_hop]), (3 * quarter, lasts[far_hop])):
        both_cores(far_hop, offset, after(block, ahead))
    for g in range(1, KVH):
        attended.append(attend(g, attended[-1]))
    earlier = [attended[-1], *swapped, *shared]
    for k, offset, block in late:
        both_cores(k, offset, after(block, *earlier))

    places = []
    for i, (k, offset, w) in enumerate(pieces):
        blocks = k if isinstance(k, tuple) else (k,)
        count = w.shape[0] // len(blocks)
        places += [(j, offset, i, n * count, count) for n, j in enumerate(blocks)]
    weights = [w for _, _, w in pieces]
    return pl.pallas_call(
        functools.partial(output_kernel, places),
        out_shape=jax.ShapeDtypeStruct((rows, width), jnp.bfloat16),
        in_specs=[VMEM] + [ANY] * (2 + len(pieces)),
        out_specs=ANY,
        scratch_shapes=[
            pltpu.VMEM((rows, NH * HD), jnp.bfloat16),
            pltpu.VMEM((NH * HD, width), jnp.bfloat16),
            pltpu.VMEM((rows, width), jnp.float32),
            pltpu.VMEM((rows, width), jnp.float32),
            pltpu.VMEM((rows, width), jnp.bfloat16),
            pltpu.SemaphoreType.DMA((4, len(places))),
            pltpu.SemaphoreType.DMA((groups,)),
            pltpu.SemaphoreType.DMA((4,)),
            pltpu.SemaphoreType.DMA((4,)),
        ],
        compiler_params=params(),
        cost_estimate=SHORT,
        name="project",
    )(post_gain.reshape(1, width), attended[-1], residual, *weights)


def solution(mesh):
    in_specs = (
        P(("req", "head"), None),
        P(),
        P(),
        P(),
        P(),
        P(),
        P("req", None),
        P(),
        P(),
        P(),
        P(),
        P("req", None, None),
        P(),
        P(),
        P(),
    )
    out_specs = P(("req", "head"), None)
    return jax.shard_map(shards, mesh=mesh, in_specs=in_specs, out_specs=out_specs, check_vma=False)
```

```python
import functools
import math

import jax
import jax.numpy as jnp
import numpy as np
from jax import lax
from jax.experimental import pallas as pl
from jax.experimental.pallas import tpu as pltpu
from jax.sharding import PartitionSpec as P

NH = 8
KVH = 2
HD = 256
REQ_DEV = 4
CH = 512
EPS = 1e-06
LOG2E = 1.4426950408889634
MASKED = -1e30
VMEM_BYTES = 64 * 1024 * 1024

SHORT = pl.CostEstimate(flops=1, bytes_accessed=1, transcendentals=0)

ANY = pl.BlockSpec(memory_space=pl.ANY)
SMEM = pl.BlockSpec(memory_space=pltpu.SMEM)
VMEM = pl.BlockSpec(memory_space=pltpu.VMEM)


def params(**more):
    return pltpu.CompilerParams(vmem_limit_bytes=VMEM_BYTES, **more)


def rope_table(rows):
    half = HD // 2
    inverse = 1000000.0 ** (-2.0 * np.arange(half) / HD)
    angle = np.arange(rows)[:, None] * inverse[None, :]
    return np.concatenate([np.cos(angle), np.sin(angle)], axis=1).astype(np.float32)


def place():
    groups = lax.axis_size("req")
    group = lax.axis_index("req").astype(jnp.int32)
    member = lax.axis_index("head").astype(jnp.int32)
    odd = group % 2
    near = group + 1 - 2 * odd
    far = lax.rem(group + 2 * odd - 1 + groups, jnp.int32(groups))
    return group, member, near, far


def slot_here(rows):
    share = CH // rows
    group, member, _, _ = place()
    return group * REQ_DEV + member // share, member % share * rows


def normalize(values):
    return values * lax.rsqrt(jnp.mean(values * values, axis=-1, keepdims=True) + EPS)


def request_of(slot_of, slot):
    return lax.fori_loop(
        0,
        slot_of.shape[0],
        lambda i, found: jnp.where(slot_of[i] == slot, i, found),
        jnp.int32(0),
    )


def mover_to(slot_of, group, target):
    def step(i, found):
        request = group * REQ_DEV + i
        return jnp.where(slot_of[request] // REQ_DEV == target, request, found)

    return lax.fori_loop(0, REQ_DEV, step, jnp.int32(0))


def pages_kernel(slot_of, page_table_in, pool, w_output, near, *rest):
    fars, pieces_out = rest[:KVH], rest[KVH : KVH + 2]
    page_table, near_held, far_held, middle, last, sems, in_sems, out_sems = rest[KVH + 2 :]
    table_copy = pltpu.make_async_copy(page_table_in, page_table, in_sems.at[0])
    table_copy.start()
    quarter = last.shape[0]
    pieces = [
        pltpu.make_async_copy(w_output.at[pl.ds(quarter, 2 * quarter)], middle, in_sems.at[1]),
        pltpu.make_async_copy(w_output.at[pl.ds(3 * quarter, quarter)], last, in_sems.at[2]),
    ]
    group, member, near_group, far_group = place()
    to_near = mover_to(slot_of, group, near_group)
    to_far = mover_to(slot_of, group, far_group)
    count, part = near.shape[0], fars[0].shape[0]
    width = 2 * HD
    table_copy.wait()
    copies = []
    for p in range(part):
        page = page_table[(member % 2) * part + p, to_far]
        copies.append(pltpu.make_async_copy(pool.at[page], far_held.at[p], sems.at[p]))
    for p in range(count):
        page = page_table[p, to_near]
        copies.append(pltpu.make_async_copy(pool.at[page], near_held.at[p], sems.at[part + p]))
    for copy in copies + pieces:
        copy.start()
    moves = []
    for p in range(part):
        copies[p].wait()
        for g in range(KVH):
            source = far_held.at[p, :, g * width : (g + 1) * width]
            moves.append(pltpu.make_async_copy(source, fars[g].at[p], out_sems.at[g, p]))
            moves[-1].start()
    for p in range(count):
        copies[part + p].wait()
        moves.append(pltpu.make_async_copy(near_held.at[p], near.at[p], out_sems.at[KVH, p]))
        moves[-1].start()
    for i, (held, out) in enumerate(zip((middle, last), pieces_out)):
        pieces[i].wait()
        moves.append(pltpu.make_async_copy(held, out, in_sems.at[1 + i]))
        moves[-1].start()
    for move in moves:
        move.wait()


def residual_kernel(gain, left, right, laurel_gain, tokens_in, out, tokens, residual, sems, out_sems):
    rows = tokens.shape[0]
    tile = 128
    tiles = rows // tile
    inputs, moves = [], []
    for i in range(tiles):
        at = slice(i * tile, (i + 1) * tile)
        inputs.append(pltpu.make_async_copy(tokens_in.at[at], tokens.at[at], sems.at[i]))
        inputs[i].start()
    for i in range(tiles):
        inputs[i].wait()
        at = slice(i * tile, (i + 1) * tile)
        x = tokens[at, :].astype(jnp.float32)
        normed = (normalize(x) * gain[...]).astype(jnp.bfloat16)
        low = lax.dot_general(
            normed, left[...], (((1,), (1,)), ((), ())), preferred_element_type=jnp.float32
        ).astype(jnp.bfloat16)
        up = jnp.dot(low, right[...], preferred_element_type=jnp.float32)
        laurel = normed.astype(jnp.float32) + normalize(up) * laurel_gain[...]
        residual[at, :] = x + laurel
        moves.append(pltpu.make_async_copy(residual.at[at], out.at[at], out_sems.at[i]))
        moves[i].start()
    for move in moves:
        move.wait()


def qkv_kernel(
    slot_of, cached_len, gain, query_gain, key_gain, tokens_in, w_query_in, w_keyval_in,
    table_in, query_out, key_out, value_out,
    tokens, w_query, w_keyval, table, table_row, normed, cosine, sine, query, key, value,
    in_sems, w_sems, out_sems,
):
    rows = tokens.shape[0]
    half = HD // 2
    chunk = min(128, rows)
    chunks = rows // chunk
    wide = 4 * HD
    tokens_copies = []
    for i in range(chunks):
        at = slice(i * chunk, (i + 1) * chunk)
        copy = pltpu.make_async_copy(tokens_in.at[at], tokens.at[at], in_sems.at[i])
        copy.start()
        tokens_copies.append(copy)
    units = [(0, c) for c in range(0, NH * HD // 2, wide)]
    units += [(1, c) for c in range(0, 2 * KVH * HD, wide)]
    units += [(0, c) for c in range(NH * HD // 2, NH * HD, wide)]
    w_copies = []
    for i, (which, c) in enumerate(units):
        source, held = ((w_query_in, w_query), (w_keyval_in, w_keyval))[which]
        columns = slice(c, c + wide)
        w_copies.append(
            pltpu.make_async_copy(source.at[:, columns], held.at[:, columns], w_sems.at[i])
        )
    w_copies[0].start()
    slot, first_row = slot_here(rows)
    start = cached_len[request_of(slot_of, slot)] + first_row
    aligned = pl.multiple_of(start // 8 * 8, 8)
    row_copy = pltpu.make_async_copy(
        table_in.at[pl.ds(aligned, 8)], table_row, in_sems.at[chunks]
    )
    row_copy.start()
    table_copy = pltpu.make_async_copy(
        table_in.at[pl.ds(0, rows)], table, in_sems.at[chunks + 1]
    )
    tile = 64
    for i in range(rows // tile):
        if i * tile % chunk == 0:
            tokens_copies[i * tile // chunk].wait()
            if i == 0:
                table_copy.start()
                w_copies[1].start()
        at = slice(i * tile, (i + 1) * tile)
        inputs = tokens[at, :].astype(jnp.float32)
        normed[at, :] = (normalize(inputs) * gain[...]).astype(jnp.bfloat16)
    row_copy.wait()
    table_copy.wait()
    base = table_row[pl.ds(start - aligned, 1), :]
    cos_base, sin_base = base[:, :half], base[:, half:]
    cos_row, sin_row = table[:, :half], table[:, half:]
    cosine[...] = cos_base * cos_row - sin_base * sin_row
    sine[...] = sin_base * cos_row + cos_base * sin_row

    sent = []
    tile = 256

    def finish(which, head, t, raw):
        at = slice(t * tile, (t + 1) * tile)
        if which == 1 and head % 2 == 1:
            held, out, place = value, value_out, head // 2
            value[place, at] = normalize(raw).astype(jnp.bfloat16)
        else:
            held, out, place = (query, query_out, head) if which == 0 else (key, key_out, head // 2)
            v = normalize(raw) * (query_gain, key_gain)[which][...]
            x, y = v[:, :half], v[:, half:]
            c, s = cosine[at], sine[at]
            held[place, at, :half] = (x * c - y * s).astype(jnp.bfloat16)
            held[place, at, half:] = (y * c + x * s).astype(jnp.bfloat16)
        if t == rows // tile - 1:
            copy = pltpu.make_async_copy(held.at[place], out.at[place], out_sems.at[len(sent)])
            copy.start()
            sent.append(copy)

    waiting = None
    for i, (which, first) in enumerate(units):
        w_copies[i].wait()
        if i + 2 < len(units):
            w_copies[i + 2].start()
        held = (w_query, w_keyval)[which]
        for c in range(first, first + wide, HD):
            for t in range(rows // tile):
                raw = jnp.dot(
                    normed[t * tile : (t + 1) * tile],
                    held[:, c : c + HD],
                    preferred_element_type=jnp.float32,
                )
                if waiting is not None:
                    finish(*waiting)
                waiting = (which, c // HD, t, raw)
    finish(*waiting)
    for copy in sent:
        copy.wait()


def attention_kernel(
    kv, slot_of, cached_len, page_table_in, query_in, key_in, value_in, pool, near, far_own,
    far_other, *rest,
):
    joined = None
    if kv == 0:
        (own_last, across_last, out_in, joined), rest = rest[:4], (None, *rest[4:])
        held, join_sems = rest[-2:]
        rest = (out_in, *rest[1:-2])
        quarter = own_last.shape[0]
        joins = [
            pltpu.make_async_copy(w, held.at[i * quarter : (i + 1) * quarter], join_sems.at[i])
            for i, w in enumerate((own_last, across_last))
        ]
        for copy in joins:
            copy.start()
    out_in, (page_table, query, key, value, out, stored, sems, in_sems, out_sems) = (
        rest[-10],
        rest[-9:],
    )
    group, member, near_group, far_group = place()
    table_copy = pltpu.make_async_copy(page_table_in, page_table, in_sems.at[3])
    table_copy.start()
    per_kv, rows = query.shape[0], query.shape[1]
    inputs = [
        pltpu.make_async_copy(query_in.at[pl.ds(kv * per_kv, per_kv)], query, in_sems.at[0]),
        pltpu.make_async_copy(key_in.at[kv], key, in_sems.at[1]),
        pltpu.make_async_copy(value_in.at[kv], value, in_sems.at[2]),
    ]
    for copy in inputs:
        copy.start()
    slot, first_row = slot_here(rows)
    request = request_of(slot_of, slot)
    length = cached_len[request]
    home = request // REQ_DEV
    page_count, page_rows = near.shape[0], near.shape[1]
    cached_rows = page_count * page_rows
    part = page_count // 2
    width = 2 * HD
    channels = slice(kv * width, (kv + 1) * width)

    def copy_page(source, p):
        return pltpu.make_async_copy(
            source, stored.at[pl.ds(p * page_rows, page_rows)], sems.at[p]
        )

    table_copy.wait()

    @pl.when(home == group)
    def _():
        for p in range(page_count):
            copy_page(pool.at[page_table[p, request], :, channels], p).start()

    @pl.when(home == near_group)
    def _():
        for p in range(page_count):
            copy_page(near.at[p, :, channels], p).start()

    @pl.when(home == far_group)
    def _():
        own_first = (member % 2) * part
        for p in range(part):
            copy_page(far_own.at[p], own_first + p).start()
            copy_page(far_other.at[p], part - own_first + p).start()

    for copy in inputs:
        copy.wait()
    for p in range(page_count):
        copy_page(near.at[p, :, channels], p).wait()

    scale = HD ** (-0.5) * LOG2E
    fresh = key.shape[0]
    tile = 256
    at_key = lax.broadcasted_iota(jnp.int32, (1, cached_rows), 1)
    bias = jnp.where(at_key < length, 0.0, MASKED)
    contract = (((1,), (1,)), ((), ()))

    def scores(h, t):
        q = query[h, t * tile : (t + 1) * tile]
        seen = fresh if fresh > rows else (t + 1) * tile
        old = lax.dot_general(q, stored[:, :HD], contract, preferred_element_type=jnp.float32)
        new = lax.dot_general(q, key[:seen], contract, preferred_element_type=jnp.float32)
        return old, new

    def finish(h, t, old, new):
        seen = new.shape[1]
        clear = 0 if fresh > rows else t * tile
        old = old + bias
        row = first_row + t * tile + lax.broadcasted_iota(jnp.int32, (tile, seen - clear), 0)
        column = clear + lax.broadcasted_iota(jnp.int32, (tile, seen - clear), 1)
        edge = jnp.where(column <= row, new[:, clear:], MASKED)
        parts = [(old, stored[:, HD:]), (edge, value[clear:seen])]
        if clear:
            parts.append((new[:, :clear], value[:clear]))
        highest = functools.reduce(
            jnp.maximum, [jnp.max(x, axis=1, keepdims=True) for x, _ in parts]
        )
        parts = [(jnp.exp2((x - highest) * scale), v) for x, v in parts]
        total = functools.reduce(jnp.add, [jnp.sum(x, axis=1, keepdims=True) for x, _ in parts])
        result = functools.reduce(
            jnp.add,
            [
                jnp.dot(x.astype(jnp.bfloat16), v, preferred_element_type=jnp.float32)
                for x, v in parts
            ],
        )
        out[h, t * tile : (t + 1) * tile] = (result / total).astype(jnp.bfloat16)

    def send(h):
        return pltpu.make_async_copy(out.at[h], out_in.at[kv * per_kv + h], out_sems.at[h])

    if joined is not None:
        for copy in joins:
            copy.wait()
        join = pltpu.make_async_copy(held, joined, join_sems.at[2])
        join.start()
    items = [(h, t) for h in range(per_kv) for t in range(rows // tile)]
    current = scores(*items[0])
    for i, (h, t) in enumerate(items):
        following = scores(*items[i + 1]) if i + 1 < len(items) else None
        finish(h, t, *current)
        current = following
        if t == rows // tile - 1:
            send(h).start()
    for h in range(per_kv):
        send(h).wait()
    if joined is not None:
        join.wait()


def output_kernel(places, post_gain, attended, residual_in, *refs):
    arrays = 1 + max(i for _, _, i, _, _ in places)
    weights, out = refs[:arrays], refs[arrays]
    lhs, held, total, residual, result, sems, lhs_sems, res_sems, out_sems = refs[-9:]
    rows, width = total.shape
    depth = refs[0].shape[0]
    per_head = HD // depth
    order = list(dict.fromkeys(k for k, *_ in places))
    wide = 512
    group = place()[0]
    lhs_copies = []
    for i, k in enumerate(order):
        block = group ^ k
        head = block // per_head
        source = attended.at[head]
        if per_head > 1:
            part = pl.multiple_of(block % per_head * depth, depth)
            source = attended.at[head, :, pl.ds(part, depth)]
        copy = pltpu.make_async_copy(
            source, lhs.at[:, i * depth : (i + 1) * depth], lhs_sems.at[i]
        )
        copy.start()
        lhs_copies.append(copy)
    copies = []
    for n in range(width // wide):
        columns = slice(n * wide, (n + 1) * wide)
        copies.append([])
        for p, (k, offset, i, row, count) in enumerate(places):
            first = order.index(k) * depth + offset
            copies[n].append(
                pltpu.make_async_copy(
                    weights[i].at[row : row + count, columns],
                    held.at[first : first + count, columns],
                    sems.at[n, p],
                )
            )
    tile = 128
    res_copies = []
    for t in range(rows // tile):
        at = slice(t * tile, (t + 1) * tile)
        res_copies.append(
            pltpu.make_async_copy(residual_in.at[at], residual.at[at], res_sems.at[t])
        )
    for copy in copies[0]:
        copy.start()
    for copy in lhs_copies:
        copy.wait()
    for copy in copies[1]:
        copy.start()
    squares = 0.0
    for n in range(width // wide):
        columns = slice(n * wide, (n + 1) * wide)
        for copy in copies[n]:
            copy.wait()
        for copy in copies[n + 2] if n + 2 < len(copies) else res_copies if n + 2 == len(copies) else []:
            copy.start()
        product = jnp.dot(lhs[...], held[:, columns], preferred_element_type=jnp.float32)
        total[:, columns] = product
        squares += jnp.sum(product * product, axis=1, keepdims=True)
    ratio = lax.rsqrt(squares * (1.0 / width) + EPS)
    out_copies = []
    for t in range(rows // tile):
        at = slice(t * tile, (t + 1) * tile)
        res_copies[t].wait()
        attn = total[at] * ratio[at] * post_gain[...]
        result[at] = ((attn + residual[at]) * (1.0 / math.sqrt(2.0))).astype(jnp.bfloat16)
        copy = pltpu.make_async_copy(result.at[at], out.at[at], out_sems.at[t])
        copy.start()
        out_copies.append(copy)
    for copy in out_copies:
        copy.wait()


def shards(
    tokens, input_gain, w_query, w_keyval, query_gain, key_gain, w_output, laurel_left,
    laurel_right, laurel_gain, post_gain, cache_pool, page_table, cached_len, slot_of,
):
    groups = lax.axis_size("req")
    members = lax.axis_size("head")
    rows, width = tokens.shape
    page_count = page_table.shape[1]
    page_rows = cache_pool.shape[1]
    channels = cache_pool.shape[2]
    share = CH // rows

    near_pairs = [(i, i ^ 1) for i in range(groups)]
    far_pairs = [(i, (i + 1) % groups if i % 2 else (i - 1) % groups) for i in range(groups)]
    def send(block, axis, pairs):
        return lax.ppermute(block, axis, pairs)

    def flip(k):
        return [(i, i ^ k) for i in range(groups)]

    def after(block, *others):
        return lax.optimization_barrier((block,) + others)[0]

    side = [(i, i ^ 1) for i in range(members)]
    far_hop = groups // 2
    top = w_output[: w_output.shape[0] // 4]
    hops = range(2, far_hop, 2)
    side = [(i, i ^ 1) for i in range(members)]
    first = {k: send(top, "req", flip(k)) for k in hops}
    first[far_hop] = send(top, "req", flip(far_hop))
    own_near = send(w_output, "req", near_pairs)
    early_done = [*first.values(), own_near]
    pages_of = page_table.T
    part = page_count // 2
    near_shape = (page_count, page_rows, channels)
    far_shape = (part, page_rows, 2 * HD)
    gain = input_gain.reshape(1, width)
    quarter = w_output.shape[0] // 4
    piece = lambda n: (n * quarter, width)
    near_out, *far_out, middle, last = pl.pallas_call(
        pages_kernel,
        out_shape=(jax.ShapeDtypeStruct(near_shape, jnp.bfloat16),)
        + (jax.ShapeDtypeStruct(far_shape, jnp.bfloat16),) * KVH
        + tuple(jax.ShapeDtypeStruct(piece(n), jnp.bfloat16) for n in (2, 1)),
        in_specs=[SMEM, ANY, ANY, ANY],
        out_specs=(ANY,) * (3 + KVH),
        scratch_shapes=[
            pltpu.SMEM(pages_of.shape, jnp.int32),
            pltpu.VMEM(near_shape, jnp.bfloat16),
            pltpu.VMEM((part, page_rows, channels), jnp.bfloat16),
            pltpu.VMEM(piece(2), jnp.bfloat16),
            pltpu.VMEM(piece(1), jnp.bfloat16),
            pltpu.SemaphoreType.DMA((page_count + part,)),
            pltpu.SemaphoreType.DMA((3,)),
            pltpu.SemaphoreType.DMA((KVH + 1, page_count)),
        ],
        compiler_params=params(),
        cost_estimate=SHORT,
        name="pages",
    )(after(slot_of, top), pages_of, cache_pool, w_output)
    near = send(after(near_out, *early_done), "req", near_pairs)

    far_out = [after(far, *early_done) for far in far_out]
    far_own = [send(far, "req", far_pairs) for far in far_out]
    middle, last = (after(w, *early_done) for w in (middle, last))
    lasts = {far_hop: send(last, "req", flip(far_hop))}
    middles = {}
    relays = {k: send(after(first[k], *early_done), "req", flip(far_hop)) for k in hops}

    table = rope_table(page_count * page_rows + CH)
    heads_shape = lambda heads: jax.ShapeDtypeStruct((heads, rows, HD), jnp.bfloat16)
    query, key, value = pl.pallas_call(
        qkv_kernel,
        out_shape=(heads_shape(NH), heads_shape(KVH), heads_shape(KVH)),
        in_specs=[SMEM, SMEM, VMEM, VMEM, VMEM, ANY, ANY, ANY, ANY],
        out_specs=(ANY,) * 3,
        scratch_shapes=[
            pltpu.VMEM((rows, width), jnp.bfloat16),
            pltpu.VMEM(w_query.shape, jnp.bfloat16),
            pltpu.VMEM(w_keyval.shape, jnp.bfloat16),
            pltpu.VMEM((rows, HD), jnp.float32),
            pltpu.VMEM((8, HD), jnp.float32),
            pltpu.VMEM((rows, width), jnp.bfloat16),
            pltpu.VMEM((rows, HD // 2), jnp.float32),
            pltpu.VMEM((rows, HD // 2), jnp.float32),
            pltpu.VMEM((NH, rows, HD), jnp.bfloat16),
            pltpu.VMEM((KVH, rows, HD), jnp.bfloat16),
            pltpu.VMEM((KVH, rows, HD), jnp.bfloat16),
            pltpu.SemaphoreType.DMA((8,)),
            pltpu.SemaphoreType.DMA((8,)),
            pltpu.SemaphoreType.DMA((NH + 2 * KVH,)),
        ],
        compiler_params=params(),
        cost_estimate=SHORT,
        name="qkv",
    )(
        slot_of, cached_len, gain, query_gain.reshape(1, HD),
        key_gain.reshape(1, HD), tokens, w_query, w_keyval, table,
    )

    far_other = [send(after(far_own[0], query), "head", side)]
    residual = pl.pallas_call(
        residual_kernel,
        out_shape=jax.ShapeDtypeStruct((rows, width), jnp.float32),
        in_specs=[VMEM] * 4 + [ANY],
        out_specs=ANY,
        scratch_shapes=[
            pltpu.VMEM((rows, width), jnp.bfloat16),
            pltpu.VMEM((rows, width), jnp.float32),
            pltpu.SemaphoreType.DMA((4,)),
            pltpu.SemaphoreType.DMA((4,)),
        ],
        compiler_params=params(),
        cost_estimate=SHORT,
        name="residual",
    )(
        gain, laurel_left.T, laurel_right, laurel_gain.reshape(1, width),
        after(tokens, far_own[0], query, near, *relays.values()),
    )
    pieces = [(0, 0, w_output), (1, 0, own_near)]
    shared = []
    for k, block in first.items():
        shared.append(send(after(block, query), "req", near_pairs))
        pieces += [(k, 0, block), (k + 1, 0, shared[-1])]
    far_other += [send(after(far, residual), "head", side) for far in far_own[1:]]
    middles[far_hop] = send(after(middle, residual, lasts[far_hop]), "req", flip(far_hop))
    for k in hops:
        middles[k] = send(after(middle, residual, *far_own), "req", flip(k))

    if share > 1:
        team = [list(range(m, m + share)) for m in range(0, members, share)]
        both = lax.all_gather(
            jnp.concatenate([key, value], axis=2), "head", axis=1, tiled=True,
            axis_index_groups=team,
        )
        key, value = both[:, :, :HD], both[:, :, HD:]

    per_kv = NH // KVH
    def attend(g, earlier=None):
        first_call = earlier is None
        more = [last, lasts[far_hop]] if first_call else [earlier]
        joined = (2 * quarter, width)
        return pl.pallas_call(
            functools.partial(attention_kernel, g),
            out_shape=(heads_shape(NH), jax.ShapeDtypeStruct(joined, jnp.bfloat16))
            if first_call
            else heads_shape(NH),
            in_specs=[SMEM] * 2 + [ANY] * (8 + len(more)),
            out_specs=(ANY, ANY) if first_call else ANY,
            scratch_shapes=[
                pltpu.SMEM(pages_of.shape, jnp.int32),
                pltpu.VMEM((per_kv, rows, HD), jnp.bfloat16),
                pltpu.VMEM((CH, HD), jnp.bfloat16),
                pltpu.VMEM((CH, HD), jnp.bfloat16),
                pltpu.VMEM((per_kv, rows, HD), jnp.bfloat16),
                pltpu.VMEM((page_count * page_rows, 2 * HD), jnp.bfloat16),
                pltpu.SemaphoreType.DMA((page_count,)),
                pltpu.SemaphoreType.DMA((4,)),
                pltpu.SemaphoreType.DMA((per_kv,)),
            ]
            + (
                [pltpu.VMEM(joined, jnp.bfloat16), pltpu.SemaphoreType.DMA((3,))]
                if first_call
                else []
            ),
            input_output_aliases={} if first_call else {10: 0},
            compiler_params=params(),
            cost_estimate=SHORT,
            name="attention",
        )(
            slot_of, cached_len, pages_of, query, key, value, cache_pool,
            near, far_own[g], far_other[g], *more,
        )

    first_heads, joined = attend(0)
    attended = [first_heads]
    late = []
    ahead = after(attended[0], *far_other[1:], *middles.values())
    swapped = []

    def both_cores(k, offset, block):
        swapped.append(send(block, "req", near_pairs))
        if isinstance(k, tuple):
            pieces.append((k, offset, block))
            pieces.append((tuple(j + 1 for j in k), offset, swapped[-1]))
        else:
            pieces.extend([(k, offset, block), (k + 1, offset, swapped[-1])])

    for k in hops:
        here = after(middles[k], ahead)
        both_cores(k, quarter, here)
        both_cores(k + far_hop, 0, after(relays[k], ahead))
        late.append((k + far_hop, quarter, send(after(middles[k], first_heads), "req", flip(far_hop))))
        both = send(joined, "req", flip(k))
        late.append(((k, k + far_hop), 3 * quarter, both))
    both_cores(far_hop, 3 * quarter, lasts[far_hop])
    both_cores(far_hop, quarter, after(middles[far_hop], ahead))
    for g in range(1, KVH):
        attended.append(attend(g, attended[-1]))
    earlier = [attended[-1], *swapped, *shared]
    for k, offset, block in late:
        both_cores(k, offset, after(block, *earlier))

    places = []
    for i, (k, offset, w) in enumerate(pieces):
        blocks = k if isinstance(k, tuple) else (k,)
        count = w.shape[0] // len(blocks)
        places += [(j, offset, i, n * count, count) for n, j in enumerate(blocks)]
    weights = [w for _, _, w in pieces]
    return pl.pallas_call(
        functools.partial(output_kernel, places),
        out_shape=jax.ShapeDtypeStruct((rows, width), jnp.bfloat16),
        in_specs=[VMEM] + [ANY] * (2 + len(pieces)),
        out_specs=ANY,
        scratch_shapes=[
            pltpu.VMEM((rows, NH * HD), jnp.bfloat16),
            pltpu.VMEM((NH * HD, width), jnp.bfloat16),
            pltpu.VMEM((rows, width), jnp.float32),
            pltpu.VMEM((rows, width), jnp.float32),
            pltpu.VMEM((rows, width), jnp.bfloat16),
            pltpu.SemaphoreType.DMA((4, len(places))),
            pltpu.SemaphoreType.DMA((groups,)),
            pltpu.SemaphoreType.DMA((4,)),
            pltpu.SemaphoreType.DMA((4,)),
        ],
        compiler_params=params(),
        cost_estimate=SHORT,
        name="project",
    )(post_gain.reshape(1, width), attended[-1], residual, *weights)


def solution(mesh):
    in_specs = (
        P(("req", "head"), None),
        P(),
        P(),
        P(),
        P(),
        P(),
        P("req", None),
        P(),
        P(),
        P(),
        P(),
        P("req", None, None),
        P(),
        P(),
        P(),
    )
    out_specs = P(("req", "head"), None)
    return jax.shard_map(shards, mesh=mesh, in_specs=in_specs, out_specs=out_specs, check_vma=False)
```

```python
import functools
import math

import jax
import jax.numpy as jnp
import numpy as np
from jax import lax
from jax.experimental import pallas as pl
from jax.experimental.pallas import tpu as pltpu
from jax.sharding import PartitionSpec as P

NH = 8
KVH = 2
HD = 256
REQ_DEV = 4
CH = 512
EPS = 1e-06
LOG2E = 1.4426950408889634
MASKED = -1e30
VMEM_BYTES = 64 * 1024 * 1024

SHORT = pl.CostEstimate(flops=1, bytes_accessed=1, transcendentals=0)

ANY = pl.BlockSpec(memory_space=pl.ANY)
SMEM = pl.BlockSpec(memory_space=pltpu.SMEM)
VMEM = pl.BlockSpec(memory_space=pltpu.VMEM)


def params(**more):
    return pltpu.CompilerParams(vmem_limit_bytes=VMEM_BYTES, **more)


def rope_table(rows):
    half = HD // 2
    inverse = 1000000.0 ** (-2.0 * np.arange(half) / HD)
    angle = np.arange(rows)[:, None] * inverse[None, :]
    return np.concatenate([np.cos(angle), np.sin(angle)], axis=1).astype(np.float32)


def place():
    groups = lax.axis_size("req")
    group = lax.axis_index("req").astype(jnp.int32)
    member = lax.axis_index("head").astype(jnp.int32)
    odd = group % 2
    near = group + 1 - 2 * odd
    far = lax.rem(group + 2 * odd - 1 + groups, jnp.int32(groups))
    return group, member, near, far


def slot_here(rows):
    share = CH // rows
    group, member, _, _ = place()
    return group * REQ_DEV + member // share, member % share * rows


def normalize(values):
    return values * lax.rsqrt(jnp.mean(values * values, axis=-1, keepdims=True) + EPS)


def request_of(slot_of, slot):
    return lax.fori_loop(
        0,
        slot_of.shape[0],
        lambda i, found: jnp.where(slot_of[i] == slot, i, found),
        jnp.int32(0),
    )


def mover_to(slot_of, group, target):
    def step(i, found):
        request = group * REQ_DEV + i
        return jnp.where(slot_of[request] // REQ_DEV == target, request, found)

    return lax.fori_loop(0, REQ_DEV, step, jnp.int32(0))


def pages_kernel(slot_of, page_table_in, pool, w_output, near, *rest):
    fars, pieces_out = rest[:KVH], rest[KVH : KVH + 2]
    page_table, near_held, far_held, middle, last, sems, in_sems, out_sems = rest[KVH + 2 :]
    table_copy = pltpu.make_async_copy(page_table_in, page_table, in_sems.at[0])
    table_copy.start()
    quarter = last.shape[0]
    pieces = [
        pltpu.make_async_copy(w_output.at[pl.ds(quarter, 2 * quarter)], middle, in_sems.at[1]),
        pltpu.make_async_copy(w_output.at[pl.ds(3 * quarter, quarter)], last, in_sems.at[2]),
    ]
    group, member, near_group, far_group = place()
    to_near = mover_to(slot_of, group, near_group)
    to_far = mover_to(slot_of, group, far_group)
    count, part = near.shape[0], fars[0].shape[0]
    width = 2 * HD
    table_copy.wait()
    copies = []
    for p in range(part):
        page = page_table[(member % 2) * part + p, to_far]
        copies.append(pltpu.make_async_copy(pool.at[page], far_held.at[p], sems.at[p]))
    for p in range(count):
        page = page_table[p, to_near]
        copies.append(pltpu.make_async_copy(pool.at[page], near_held.at[p], sems.at[part + p]))
    for copy in copies + pieces:
        copy.start()
    moves = []
    for p in range(part):
        copies[p].wait()
        for g in range(KVH):
            source = far_held.at[p, :, g * width : (g + 1) * width]
            moves.append(pltpu.make_async_copy(source, fars[g].at[p], out_sems.at[g, p]))
            moves[-1].start()
    for p in range(count):
        copies[part + p].wait()
        moves.append(pltpu.make_async_copy(near_held.at[p], near.at[p], out_sems.at[KVH, p]))
        moves[-1].start()
    for i, (held, out) in enumerate(zip((middle, last), pieces_out)):
        pieces[i].wait()
        moves.append(pltpu.make_async_copy(held, out, in_sems.at[1 + i]))
        moves[-1].start()
    for move in moves:
        move.wait()


def residual_kernel(gain, left, right, laurel_gain, tokens_in, out, tokens, residual, sems, out_sems):
    rows = tokens.shape[0]
    tile = 128
    tiles = rows // tile
    inputs, moves = [], []
    for i in range(tiles):
        at = slice(i * tile, (i + 1) * tile)
        inputs.append(pltpu.make_async_copy(tokens_in.at[at], tokens.at[at], sems.at[i]))
        inputs[i].start()
    for i in range(tiles):
        inputs[i].wait()
        at = slice(i * tile, (i + 1) * tile)
        x = tokens[at, :].astype(jnp.float32)
        normed = (normalize(x) * gain[...]).astype(jnp.bfloat16)
        low = lax.dot_general(
            normed, left[...], (((1,), (1,)), ((), ())), preferred_element_type=jnp.float32
        ).astype(jnp.bfloat16)
        up = jnp.dot(low, right[...], preferred_element_type=jnp.float32)
        laurel = normed.astype(jnp.float32) + normalize(up) * laurel_gain[...]
        residual[at, :] = x + laurel
        moves.append(pltpu.make_async_copy(residual.at[at], out.at[at], out_sems.at[i]))
        moves[i].start()
    for move in moves:
        move.wait()


def qkv_kernel(
    slot_of, cached_len, gain, query_gain, key_gain, tokens_in, w_query_in, w_keyval_in,
    table_in, query_out, key_out, value_out,
    tokens, w_query, w_keyval, table, table_row, normed, cosine, sine, query, key, value,
    in_sems, w_sems, out_sems,
):
    rows = tokens.shape[0]
    half = HD // 2
    chunk = min(128, rows)
    chunks = rows // chunk
    wide = 4 * HD
    tokens_copies = []
    for i in range(chunks):
        at = slice(i * chunk, (i + 1) * chunk)
        copy = pltpu.make_async_copy(tokens_in.at[at], tokens.at[at], in_sems.at[i])
        copy.start()
        tokens_copies.append(copy)
    units = [(0, c) for c in range(0, NH * HD // 2, wide)]
    units += [(1, c) for c in range(0, 2 * KVH * HD, wide)]
    units += [(0, c) for c in range(NH * HD // 2, NH * HD, wide)]
    w_copies = []
    for i, (which, c) in enumerate(units):
        source, held = ((w_query_in, w_query), (w_keyval_in, w_keyval))[which]
        columns = slice(c, c + wide)
        w_copies.append(
            pltpu.make_async_copy(source.at[:, columns], held.at[:, columns], w_sems.at[i])
        )
    w_copies[0].start()
    slot, first_row = slot_here(rows)
    start = cached_len[request_of(slot_of, slot)] + first_row
    aligned = pl.multiple_of(start // 8 * 8, 8)
    row_copy = pltpu.make_async_copy(
        table_in.at[pl.ds(aligned, 8)], table_row, in_sems.at[chunks]
    )
    row_copy.start()
    table_copy = pltpu.make_async_copy(
        table_in.at[pl.ds(0, rows)], table, in_sems.at[chunks + 1]
    )
    tile = 64
    for i in range(rows // tile):
        if i * tile % chunk == 0:
            tokens_copies[i * tile // chunk].wait()
            if i == 0:
                table_copy.start()
                w_copies[1].start()
        at = slice(i * tile, (i + 1) * tile)
        inputs = tokens[at, :].astype(jnp.float32)
        normed[at, :] = (normalize(inputs) * gain[...]).astype(jnp.bfloat16)
    row_copy.wait()
    table_copy.wait()
    base = table_row[pl.ds(start - aligned, 1), :]
    cos_base, sin_base = base[:, :half], base[:, half:]
    cos_row, sin_row = table[:, :half], table[:, half:]
    cosine[...] = cos_base * cos_row - sin_base * sin_row
    sine[...] = sin_base * cos_row + cos_base * sin_row

    sent = []
    tile = 256

    def finish(which, head, t, raw):
        at = slice(t * tile, (t + 1) * tile)
        if which == 1 and head % 2 == 1:
            held, out, place = value, value_out, head // 2
            value[place, at] = normalize(raw).astype(jnp.bfloat16)
        else:
            held, out, place = (query, query_out, head) if which == 0 else (key, key_out, head // 2)
            v = normalize(raw) * (query_gain, key_gain)[which][...]
            x, y = v[:, :half], v[:, half:]
            c, s = cosine[at], sine[at]
            held[place, at, :half] = (x * c - y * s).astype(jnp.bfloat16)
            held[place, at, half:] = (y * c + x * s).astype(jnp.bfloat16)
        if t == rows // tile - 1:
            copy = pltpu.make_async_copy(held.at[place], out.at[place], out_sems.at[len(sent)])
            copy.start()
            sent.append(copy)

    waiting = None
    for i, (which, first) in enumerate(units):
        w_copies[i].wait()
        if i + 2 < len(units):
            w_copies[i + 2].start()
        held = (w_query, w_keyval)[which]
        for c in range(first, first + wide, HD):
            for t in range(rows // tile):
                raw = jnp.dot(
                    normed[t * tile : (t + 1) * tile],
                    held[:, c : c + HD],
                    preferred_element_type=jnp.float32,
                )
                if waiting is not None:
                    finish(*waiting)
                waiting = (which, c // HD, t, raw)
    finish(*waiting)
    for copy in sent:
        copy.wait()


def attention_kernel(
    kv, slot_of, cached_len, page_table_in, query_in, key_in, value_in, pool, near, far_own,
    far_other, *rest,
):
    joined = None
    if kv == 0:
        (own_last, across_last, out_in, joined), rest = rest[:4], (None, *rest[4:])
        held, join_sems = rest[-2:]
        rest = (out_in, *rest[1:-2])
        quarter = own_last.shape[0]
        joins = [
            pltpu.make_async_copy(w, held.at[i * quarter : (i + 1) * quarter], join_sems.at[i])
            for i, w in enumerate((own_last, across_last))
        ]
        for copy in joins:
            copy.start()
    out_in, (page_table, query, key, value, out, stored, sems, in_sems, out_sems) = (
        rest[-10],
        rest[-9:],
    )
    group, member, near_group, far_group = place()
    table_copy = pltpu.make_async_copy(page_table_in, page_table, in_sems.at[3])
    table_copy.start()
    per_kv, rows = query.shape[0], query.shape[1]
    inputs = [
        pltpu.make_async_copy(query_in.at[pl.ds(kv * per_kv, per_kv)], query, in_sems.at[0]),
        pltpu.make_async_copy(key_in.at[kv], key, in_sems.at[1]),
        pltpu.make_async_copy(value_in.at[kv], value, in_sems.at[2]),
    ]
    for copy in inputs:
        copy.start()
    slot, first_row = slot_here(rows)
    request = request_of(slot_of, slot)
    length = cached_len[request]
    home = request // REQ_DEV
    page_count, page_rows = near.shape[0], near.shape[1]
    cached_rows = page_count * page_rows
    part = page_count // 2
    width = 2 * HD
    channels = slice(kv * width, (kv + 1) * width)

    def copy_page(source, p):
        return pltpu.make_async_copy(
            source, stored.at[pl.ds(p * page_rows, page_rows)], sems.at[p]
        )

    table_copy.wait()

    @pl.when(home == group)
    def _():
        for p in range(page_count):
            copy_page(pool.at[page_table[p, request], :, channels], p).start()

    @pl.when(home == near_group)
    def _():
        for p in range(page_count):
            copy_page(near.at[p, :, channels], p).start()

    @pl.when(home == far_group)
    def _():
        own_first = (member % 2) * part
        for p in range(part):
            copy_page(far_own.at[p], own_first + p).start()
            copy_page(far_other.at[p], part - own_first + p).start()

    for copy in inputs:
        copy.wait()
    for p in range(page_count):
        copy_page(near.at[p, :, channels], p).wait()

    scale = HD ** (-0.5) * LOG2E
    fresh = key.shape[0]
    tile = 256
    at_key = lax.broadcasted_iota(jnp.int32, (1, cached_rows), 1)
    bias = jnp.where(at_key < length, 0.0, MASKED)
    contract = (((1,), (1,)), ((), ()))

    def scores(h, t):
        q = query[h, t * tile : (t + 1) * tile]
        seen = fresh if fresh > rows else (t + 1) * tile
        old = lax.dot_general(q, stored[:, :HD], contract, preferred_element_type=jnp.float32)
        new = lax.dot_general(q, key[:seen], contract, preferred_element_type=jnp.float32)
        return old, new

    def finish(h, t, old, new):
        seen = new.shape[1]
        clear = 0 if fresh > rows else t * tile
        old = old + bias
        row = first_row + t * tile + lax.broadcasted_iota(jnp.int32, (tile, seen - clear), 0)
        column = clear + lax.broadcasted_iota(jnp.int32, (tile, seen - clear), 1)
        edge = jnp.where(column <= row, new[:, clear:], MASKED)
        parts = [(old, stored[:, HD:]), (edge, value[clear:seen])]
        if clear:
            parts.append((new[:, :clear], value[:clear]))
        highest = functools.reduce(
            jnp.maximum, [jnp.max(x, axis=1, keepdims=True) for x, _ in parts]
        )
        parts = [(jnp.exp2((x - highest) * scale), v) for x, v in parts]
        total = functools.reduce(jnp.add, [jnp.sum(x, axis=1, keepdims=True) for x, _ in parts])
        result = functools.reduce(
            jnp.add,
            [
                jnp.dot(x.astype(jnp.bfloat16), v, preferred_element_type=jnp.float32)
                for x, v in parts
            ],
        )
        out[h, t * tile : (t + 1) * tile] = (result / total).astype(jnp.bfloat16)

    def send(h):
        return pltpu.make_async_copy(out.at[h], out_in.at[kv * per_kv + h], out_sems.at[h])

    if joined is not None:
        for copy in joins:
            copy.wait()
        join = pltpu.make_async_copy(held, joined, join_sems.at[2])
        join.start()
    items = [(h, t) for h in range(per_kv) for t in range(rows // tile)]
    current = scores(*items[0])
    for i, (h, t) in enumerate(items):
        following = scores(*items[i + 1]) if i + 1 < len(items) else None
        finish(h, t, *current)
        current = following
        if t == rows // tile - 1:
            send(h).start()
    for h in range(per_kv):
        send(h).wait()
    if joined is not None:
        join.wait()


def output_kernel(places, post_gain, attended, residual_in, *refs):
    arrays = 1 + max(i for _, _, i, _, _ in places)
    weights, out = refs[:arrays], refs[arrays]
    lhs, held, total, residual, result, sems, lhs_sems, res_sems, out_sems = refs[-9:]
    rows, width = total.shape
    depth = refs[0].shape[0]
    per_head = HD // depth
    order = list(dict.fromkeys(k for k, *_ in places))
    wide = 512
    group = place()[0]
    lhs_copies = []
    for i, k in enumerate(order):
        block = group ^ k
        head = block // per_head
        source = attended.at[head]
        if per_head > 1:
            part = pl.multiple_of(block % per_head * depth, depth)
            source = attended.at[head, :, pl.ds(part, depth)]
        copy = pltpu.make_async_copy(
            source, lhs.at[:, i * depth : (i + 1) * depth], lhs_sems.at[i]
        )
        copy.start()
        lhs_copies.append(copy)
    copies = []
    for n in range(width // wide):
        columns = slice(n * wide, (n + 1) * wide)
        copies.append([])
        for p, (k, offset, i, row, count) in enumerate(places):
            first = order.index(k) * depth + offset
            copies[n].append(
                pltpu.make_async_copy(
                    weights[i].at[row : row + count, columns],
                    held.at[first : first + count, columns],
                    sems.at[n, p],
                )
            )
    tile = 128
    res_copies = []
    for t in range(rows // tile):
        at = slice(t * tile, (t + 1) * tile)
        res_copies.append(
            pltpu.make_async_copy(residual_in.at[at], residual.at[at], res_sems.at[t])
        )
    for copy in copies[0]:
        copy.start()
    for copy in lhs_copies:
        copy.wait()
    for copy in copies[1]:
        copy.start()
    squares = 0.0
    for n in range(width // wide):
        columns = slice(n * wide, (n + 1) * wide)
        for copy in copies[n]:
            copy.wait()
        for copy in copies[n + 2] if n + 2 < len(copies) else res_copies if n + 2 == len(copies) else []:
            copy.start()
        product = jnp.dot(lhs[...], held[:, columns], preferred_element_type=jnp.float32)
        total[:, columns] = product
        squares += jnp.sum(product * product, axis=1, keepdims=True)
    ratio = lax.rsqrt(squares * (1.0 / width) + EPS)
    out_copies = []
    for t in range(rows // tile):
        at = slice(t * tile, (t + 1) * tile)
        res_copies[t].wait()
        attn = total[at] * ratio[at] * post_gain[...]
        result[at] = ((attn + residual[at]) * (1.0 / math.sqrt(2.0))).astype(jnp.bfloat16)
        copy = pltpu.make_async_copy(result.at[at], out.at[at], out_sems.at[t])
        copy.start()
        out_copies.append(copy)
    for copy in out_copies:
        copy.wait()


def shards(
    tokens, input_gain, w_query, w_keyval, query_gain, key_gain, w_output, laurel_left,
    laurel_right, laurel_gain, post_gain, cache_pool, page_table, cached_len, slot_of,
):
    groups = lax.axis_size("req")
    members = lax.axis_size("head")
    rows, width = tokens.shape
    page_count = page_table.shape[1]
    page_rows = cache_pool.shape[1]
    channels = cache_pool.shape[2]
    share = CH // rows

    near_pairs = [(i, i ^ 1) for i in range(groups)]
    far_pairs = [(i, (i + 1) % groups if i % 2 else (i - 1) % groups) for i in range(groups)]
    def send(block, axis, pairs):
        return lax.ppermute(block, axis, pairs)

    def flip(k):
        return [(i, i ^ k) for i in range(groups)]

    def after(block, *others):
        return lax.optimization_barrier((block,) + others)[0]

    side = [(i, i ^ 1) for i in range(members)]
    far_hop = groups // 2
    top = w_output[: w_output.shape[0] // 4]
    hops = range(2, far_hop, 2)
    side = [(i, i ^ 1) for i in range(members)]
    first = {k: send(top, "req", flip(k)) for k in hops}
    first[far_hop] = send(top, "req", flip(far_hop))
    own_near = send(w_output, "req", near_pairs)
    early_done = [*first.values(), own_near]
    pages_of = page_table.T
    part = page_count // 2
    near_shape = (page_count, page_rows, channels)
    far_shape = (part, page_rows, 2 * HD)
    gain = input_gain.reshape(1, width)
    quarter = w_output.shape[0] // 4
    piece = lambda n: (n * quarter, width)
    near_out, *far_out, middle, last = pl.pallas_call(
        pages_kernel,
        out_shape=(jax.ShapeDtypeStruct(near_shape, jnp.bfloat16),)
        + (jax.ShapeDtypeStruct(far_shape, jnp.bfloat16),) * KVH
        + tuple(jax.ShapeDtypeStruct(piece(n), jnp.bfloat16) for n in (2, 1)),
        in_specs=[SMEM, ANY, ANY, ANY],
        out_specs=(ANY,) * (3 + KVH),
        scratch_shapes=[
            pltpu.SMEM(pages_of.shape, jnp.int32),
            pltpu.VMEM(near_shape, jnp.bfloat16),
            pltpu.VMEM((part, page_rows, channels), jnp.bfloat16),
            pltpu.VMEM(piece(2), jnp.bfloat16),
            pltpu.VMEM(piece(1), jnp.bfloat16),
            pltpu.SemaphoreType.DMA((page_count + part,)),
            pltpu.SemaphoreType.DMA((3,)),
            pltpu.SemaphoreType.DMA((KVH + 1, page_count)),
        ],
        compiler_params=params(),
        cost_estimate=SHORT,
        name="pages",
    )(after(slot_of, top), pages_of, cache_pool, w_output)
    near = send(after(near_out, *early_done), "req", near_pairs)

    far_out = [after(far, *early_done) for far in far_out]
    far_own = [send(far, "req", far_pairs) for far in far_out]
    middle, last = (after(w, *early_done) for w in (middle, last))
    lasts = {far_hop: send(last, "req", flip(far_hop))}
    middles = {}
    relays = {k: send(after(first[k], *early_done), "req", flip(far_hop)) for k in hops}

    table = rope_table(page_count * page_rows + CH)
    heads_shape = lambda heads: jax.ShapeDtypeStruct((heads, rows, HD), jnp.bfloat16)
    query, key, value = pl.pallas_call(
        qkv_kernel,
        out_shape=(heads_shape(NH), heads_shape(KVH), heads_shape(KVH)),
        in_specs=[SMEM, SMEM, VMEM, VMEM, VMEM, ANY, ANY, ANY, ANY],
        out_specs=(ANY,) * 3,
        scratch_shapes=[
            pltpu.VMEM((rows, width), jnp.bfloat16),
            pltpu.VMEM(w_query.shape, jnp.bfloat16),
            pltpu.VMEM(w_keyval.shape, jnp.bfloat16),
            pltpu.VMEM((rows, HD), jnp.float32),
            pltpu.VMEM((8, HD), jnp.float32),
            pltpu.VMEM((rows, width), jnp.bfloat16),
            pltpu.VMEM((rows, HD // 2), jnp.float32),
            pltpu.VMEM((rows, HD // 2), jnp.float32),
            pltpu.VMEM((NH, rows, HD), jnp.bfloat16),
            pltpu.VMEM((KVH, rows, HD), jnp.bfloat16),
            pltpu.VMEM((KVH, rows, HD), jnp.bfloat16),
            pltpu.SemaphoreType.DMA((8,)),
            pltpu.SemaphoreType.DMA((8,)),
            pltpu.SemaphoreType.DMA((NH + 2 * KVH,)),
        ],
        compiler_params=params(),
        cost_estimate=SHORT,
        name="qkv",
    )(
        slot_of, cached_len, gain, query_gain.reshape(1, HD),
        key_gain.reshape(1, HD), tokens, w_query, w_keyval, table,
    )

    far_other = [send(after(far_own[0], query), "head", side)]
    residual = pl.pallas_call(
        residual_kernel,
        out_shape=jax.ShapeDtypeStruct((rows, width), jnp.float32),
        in_specs=[VMEM] * 4 + [ANY],
        out_specs=ANY,
        scratch_shapes=[
            pltpu.VMEM((rows, width), jnp.bfloat16),
            pltpu.VMEM((rows, width), jnp.float32),
            pltpu.SemaphoreType.DMA((4,)),
            pltpu.SemaphoreType.DMA((4,)),
        ],
        compiler_params=params(),
        cost_estimate=SHORT,
        name="residual",
    )(
        gain, laurel_left.T, laurel_right, laurel_gain.reshape(1, width),
        after(tokens, far_own[0], query, near, *relays.values()),
    )
    pieces = [(0, 0, w_output), (1, 0, own_near)]
    shared = []
    for k, block in first.items():
        shared.append(send(after(block, query), "req", near_pairs))
        pieces += [(k, 0, block), (k + 1, 0, shared[-1])]
    far_other += [send(after(far, residual), "head", side) for far in far_own[1:]]
    middles[far_hop] = send(after(middle, residual, lasts[far_hop]), "req", flip(far_hop))
    for k in hops:
        middles[k] = send(after(middle, residual, *far_own), "req", flip(k))

    if share > 1:
        team = [list(range(m, m + share)) for m in range(0, members, share)]
        both = lax.all_gather(
            jnp.concatenate([key, value], axis=2), "head", axis=1, tiled=True,
            axis_index_groups=team,
        )
        key, value = both[:, :, :HD], both[:, :, HD:]

    per_kv = NH // KVH
    def attend(g, earlier=None):
        first_call = earlier is None
        more = [last, lasts[far_hop]] if first_call else [earlier]
        joined = (2 * quarter, width)
        return pl.pallas_call(
            functools.partial(attention_kernel, g),
            out_shape=(heads_shape(NH), jax.ShapeDtypeStruct(joined, jnp.bfloat16))
            if first_call
            else heads_shape(NH),
            in_specs=[SMEM] * 2 + [ANY] * (8 + len(more)),
            out_specs=(ANY, ANY) if first_call else ANY,
            scratch_shapes=[
                pltpu.SMEM(pages_of.shape, jnp.int32),
                pltpu.VMEM((per_kv, rows, HD), jnp.bfloat16),
                pltpu.VMEM((CH, HD), jnp.bfloat16),
                pltpu.VMEM((CH, HD), jnp.bfloat16),
                pltpu.VMEM((per_kv, rows, HD), jnp.bfloat16),
                pltpu.VMEM((page_count * page_rows, 2 * HD), jnp.bfloat16),
                pltpu.SemaphoreType.DMA((page_count,)),
                pltpu.SemaphoreType.DMA((4,)),
                pltpu.SemaphoreType.DMA((per_kv,)),
            ]
            + (
                [pltpu.VMEM(joined, jnp.bfloat16), pltpu.SemaphoreType.DMA((3,))]
                if first_call
                else []
            ),
            input_output_aliases={} if first_call else {10: 0},
            compiler_params=params(),
            cost_estimate=SHORT,
            name="attention",
        )(
            slot_of, cached_len, pages_of, query, key, value, cache_pool,
            near, far_own[g], far_other[g], *more,
        )

    first_heads, joined = attend(0)
    attended = [first_heads]
    late = []
    ahead = after(attended[0], *far_other[1:], *middles.values())
    swapped = []

    def both_cores(k, offset, block):
        swapped.append(send(block, "req", near_pairs))
        if isinstance(k, tuple):
            pieces.append((k, offset, block))
            pieces.append((tuple(j + 1 for j in k), offset, swapped[-1]))
        else:
            pieces.extend([(k, offset, block), (k + 1, offset, swapped[-1])])

    for k in hops:
        here = after(middles[k], ahead)
        both_cores(k, quarter, here)
        late.append((k + far_hop, quarter, send(after(middles[k], first_heads), "req", flip(far_hop))))
        both = send(joined, "req", flip(k))
        late.append(((k, k + far_hop), 3 * quarter, both))
    both_cores(far_hop, 3 * quarter, lasts[far_hop])
    for g in range(1, KVH):
        attended.append(attend(g, attended[-1]))
    earlier = [attended[-1], *swapped, *shared]
    for k in hops:
        both_cores(k + far_hop, 0, after(relays[k], attended[-1]))
    both_cores(far_hop, quarter, after(middles[far_hop], attended[-1]))
    for k, offset, block in late:
        both_cores(k, offset, after(block, *earlier))

    places = []
    for i, (k, offset, w) in enumerate(pieces):
        blocks = k if isinstance(k, tuple) else (k,)
        count = w.shape[0] // len(blocks)
        places += [(j, offset, i, n * count, count) for n, j in enumerate(blocks)]
    weights = [w for _, _, w in pieces]
    return pl.pallas_call(
        functools.partial(output_kernel, places),
        out_shape=jax.ShapeDtypeStruct((rows, width), jnp.bfloat16),
        in_specs=[VMEM] + [ANY] * (2 + len(pieces)),
        out_specs=ANY,
        scratch_shapes=[
            pltpu.VMEM((rows, NH * HD), jnp.bfloat16),
            pltpu.VMEM((NH * HD, width), jnp.bfloat16),
            pltpu.VMEM((rows, width), jnp.float32),
            pltpu.VMEM((rows, width), jnp.float32),
            pltpu.VMEM((rows, width), jnp.bfloat16),
            pltpu.SemaphoreType.DMA((4, len(places))),
            pltpu.SemaphoreType.DMA((groups,)),
            pltpu.SemaphoreType.DMA((4,)),
            pltpu.SemaphoreType.DMA((4,)),
        ],
        compiler_params=params(),
        cost_estimate=SHORT,
        name="project",
    )(post_gain.reshape(1, width), attended[-1], residual, *weights)


def solution(mesh):
    in_specs = (
        P(("req", "head"), None),
        P(),
        P(),
        P(),
        P(),
        P(),
        P("req", None),
        P(),
        P(),
        P(),
        P(),
        P("req", None, None),
        P(),
        P(),
        P(),
    )
    out_specs = P(("req", "head"), None)
    return jax.shard_map(shards, mesh=mesh, in_specs=in_specs, out_specs=out_specs, check_vma=False)
```
